512 devices in a mesh: hull: 256 (over x, y, z), fn: 2 (over core).
Axes of the slice: x: 4, y: 8, z: 8, core: 2. Of those that a mesh axis runs over, the one named last changes fastest.
Arguments:
- adj_rhs: float32 [4096, 64, 128], P('hull', 'fn'), may hold values from -6 to 6
- psi_init: float32 [4096, 64, 128], P('hull', 'fn'), may hold values from -6 to 6
- couple: bfloat16 [4096, 6, 128, 128], P('hull'), may hold values from -0.109375 to 0.109375
- diag_inv: bfloat16 [4096, 128, 128], P('hull')
- neighbours: int32 [4096, 6], P('hull'), may hold values from 0 to 4095, as said below
- sens: bfloat16 [4096, 16, 128], P('hull'), may hold values from -0.125 to 0.125
- owner: int32 [4096, 16], P('hull'), may hold values from 0 to 4095, as said below
Outputs:
- adjoint: float32 [4096, 64, 128], P('hull', 'fn')
- grad: float32 [4096, 64], P(('hull', 'fn'))
The draws below stay inside these ranges and needn't reach their ends.
Inputs may be any that keep to these rules, and one draw needn't show every extreme that they name: `neighbours`: every neighbour of block row i lies within 2 block rows of i, and the distance 2 occurs. `owner`: the slots below 8 of block b name coordinates within 8 of b (coordinate b sits at block b's position along the hull), and the distance 8 occurs; the other slots may name any coordinate.
All inputs are finite; a program needn't handle non-finite values.
Results may differ from the reference program's by a relative error of at most 0.0049.
Values may be sent and summed in bfloat16 or wider, within the bound.
A program may use at most 64 MiB of HBM per device.

```python
import jax
import jax.numpy as jnp
from jax import lax

ROWS = 128
NBR = 6
FNS = 64
NCOORD = 4096
KLOC = 16
WIN = 8
REACH = 2
SWEEPS = 3
NBLK = 4096


def draw_diag_inv(key, part):
    key = jax.random.fold_in(key, 11)
    noise = jax.random.normal(key, (NBLK, ROWS, ROWS), jnp.float32)
    eye = jnp.eye(ROWS, dtype=jnp.float32)[None]
    return (eye + noise * (0.5 / ROWS ** 0.5)).astype(jnp.bfloat16)


def draw_neighbours(key, part):
    key = jax.random.fold_in(key, 23)
    key_sign, key_size = jax.random.split(key)
    signs = jax.random.randint(key_sign, (NBLK, NBR), 0, 2) * 2 - 1
    sizes = jax.random.randint(key_size, (NBLK, NBR), 1, REACH + 1)
    rows = jnp.arange(NBLK, dtype=jnp.int32)[:, None]
    index = jnp.clip(rows + signs * sizes, 0, NBLK - 1).astype(jnp.int32)
    index = index.at[0, 0].set(REACH)
    index = index.at[NBLK - 1, 0].set(NBLK - 1 - REACH)
    return index


def draw_owner(key, part):
    key = jax.random.fold_in(key, 37)
    key_near, key_far = jax.random.split(key)
    half_slots = KLOC // 2
    offsets = jax.random.randint(key_near, (NBLK, half_slots), -WIN, WIN + 1)
    middle = NBLK // 2
    offsets = offsets.at[middle, 0].set(WIN)
    rows = jnp.arange(NBLK, dtype=jnp.int32)[:, None]
    centre = rows * NCOORD // NBLK
    near = jnp.clip(centre + offsets, 0, NCOORD - 1).astype(jnp.int32)
    far = jax.random.randint(key_far, (NBLK, KLOC - half_slots), 0, NCOORD).astype(jnp.int32)
    far = far.at[0, KLOC - half_slots - 1].set(NCOORD - 1)
    far = far.at[1, KLOC - half_slots - 1].set(0)
    return jnp.concatenate([near, far], axis=1).astype(jnp.int32)


def levels(rng, shape, cuts, low, largest):
    loudness = 1.0
    for position, shards_of in cuts:
        steps = jax.random.uniform(jax.random.fold_in(jax.random.fold_in(rng, 6), position), (shards_of,), jnp.float32, low / len(cuts), largest / len(cuts))
        loudness = loudness * jnp.repeat(jnp.exp(steps), shape[position] // shards_of).reshape((-1,) + (1,) * (len(shape) - 1 - position))
    return loudness


def gaussian(stream_key, shape, scale, most, pieces=(), kind=jnp.bfloat16):
    array = scale * jax.random.normal(stream_key, shape, jnp.float32)
    if pieces:
        array = array * levels(stream_key, shape, pieces, -0.22, 0.18)
    return jnp.clip(array, -most, most).astype(kind)


def setup_inputs(seed: int = 0) -> dict:
    seeds = jax.random.split(jax.random.key(seed), 8)
    adj_rhs = gaussian(seeds[0], (NBLK, FNS, ROWS), 1.0, 6.0, ((0, 256), (1, 2)), jnp.float32)
    psi_init = gaussian(seeds[1], (NBLK, FNS, ROWS), 1.0, 6.0, ((0, 256), (1, 2)), jnp.float32)
    couple = gaussian(seeds[2], (NBLK, NBR, ROWS, ROWS), (ROWS * 24) ** -0.5, 0.109375, ((0, 256),))
    diag_inv = draw_diag_inv(jax.random.fold_in(seeds[7], 71), 0)
    neighbours = draw_neighbours(jax.random.fold_in(seeds[7], 71), 0)
    sens = gaussian(seeds[5], (NBLK, KLOC, ROWS), (ROWS * max(1, NBLK * KLOC // NCOORD)) ** -0.5, 0.125, ((0, 256),))
    owner = draw_owner(jax.random.fold_in(seeds[7], 71), 0)
    return {"adj_rhs": adj_rhs, "psi_init": psi_init, "couple": couple, "diag_inv": diag_inv, "neighbours": neighbours, "sens": sens, "owner": owner}


def reference(adj_rhs, psi_init, couple, diag_inv, neighbours, sens, owner):
    psi = psi_init
    for sweep_step in range(SWEEPS):
        lagged = psi.astype(jnp.bfloat16)
        coupled = jnp.zeros(psi.shape, jnp.float32)
        for slot in range(NBR):
            nearby = lax.optimization_barrier(lagged[neighbours[:, slot]]).astype(jnp.float32)
            coupled = coupled + jnp.einsum("bfr,brs->bfs", nearby, couple[:, slot].astype(jnp.float32))
        updated = lax.optimization_barrier((adj_rhs - coupled).astype(jnp.bfloat16)).astype(jnp.float32)
        psi = jnp.einsum("bfr,brs->bfs", updated, diag_inv.astype(jnp.float32))
    final = lax.optimization_barrier(psi.astype(jnp.bfloat16)).astype(jnp.float32)
    contrib = -jnp.einsum("bfr,bmr->bmf", final, sens.astype(jnp.float32))
    grad = jax.ops.segment_sum(contrib.reshape(-1, FNS), owner.reshape(-1), num_segments=NCOORD)
    return psi, grad
```

```python
import functools

import jax
import jax.numpy as jnp
from jax import lax
from jax.experimental import pallas as pl
from jax.experimental.pallas import tpu as pltpu
from jax.sharding import PartitionSpec as P

MESH = pl.DeviceIdType.MESH
BF, F32, I32 = jnp.bfloat16, jnp.float32, jnp.int32
NX, NY, NZ = 4, 8, 8
B = 16
FN = 32
R = 128
NBR, KLOC, SWEEPS, REACH = 6, 16, 3, 2
GROUPS = ((2, 6), (6, 10), (10, 14), (0, 2), (14, 16))


def dot(a, b):
    return jnp.dot(a, b, preferred_element_type=F32)


def iota(shape, dim):
    return lax.broadcasted_iota(I32, shape, dim)


def lane_of(coordinate):
    y = (coordinate // (NZ * 16)) % NY
    core = (coordinate >> 3) & 1
    return (coordinate & 3) * 32 + y * 4 + core * 2 + ((coordinate >> 2) & 1)


def kernel(
    rhs_hbm, psi_hbm, couple_hbm, diag_hbm, nbr_hbm, sens_hbm, owner_hbm,
    adj_hbm, grad_ref,
    rhs, psi, couple, diag, nbr, sens, owner, adj,
    local0, local1, local2, edge0, edge1, edge2, st, tgt, oh, ohn, crecv, nsend, nrecv, dsend, xrecv, psend, precv,
    load_sem, weight_sem, out_sem, halo_s, halo_r, tgt_s, tgt_r, c_s, c_r, n_s, n_r, x_s, x_r, p_s, p_r,
):
    local, edge = (local0, local1, local2), (edge0, edge1, edge2)
    h = lax.axis_index("hull")
    core = lax.axis_index("fn")
    n_hull = NX * NY * NZ
    x, y, z = h // (NY * NZ), (h // NZ) % NY, h % NZ

    def device(i, j, k, c):
        return ((i * NY + j) * NZ + k, c)

    right, left = ((h + 1) % n_hull, core), ((h + n_hull - 1) % n_hull, core)
    z_peers = [device(x, y, (z + k) % NZ, core) for k in range(1, NZ)]
    x_peers = [device((x + k) % NX, y, z, core) for k in range(1, NX)]
    yc = [(k, e) for e in range(2) for k in range(NY) if (k, e) != (0, 0)]
    yc_peers = [device(x, (y + k) % NY, z, (core + e) % 2) for k, e in yc]

    barrier = pltpu.get_barrier_semaphore()
    everyone = [right, left] + z_peers + x_peers + yc_peers
    for peer in everyone:
        pl.semaphore_signal(barrier, inc=1, device_id=peer, device_id_type=MESH)

    loads = {}

    def load(name, source, target):
        loads[name] = pltpu.make_async_copy(source, target, load_sem.at[len(loads)])
        loads[name].start()

    load("psi0", psi_hbm.at[pl.ds(0, 2)], psi.at[pl.ds(0, 2)])
    load("psi1", psi_hbm.at[pl.ds(B - 2, 2)], psi.at[pl.ds(B - 2, 2)])
    load("owner", owner_hbm, owner)
    load("psi", psi_hbm.at[pl.ds(2, B - 4)], psi.at[pl.ds(2, B - 4)])
    load("nbr", nbr_hbm, nbr)
    load("rhs", rhs_hbm, rhs)
    weights = []
    for g, (a, b) in enumerate(GROUPS):
        rows = pl.ds(a, b - a)
        weights.append((
            pltpu.make_async_copy(couple_hbm.at[rows], couple.at[rows], weight_sem.at[2 * g]),
            pltpu.make_async_copy(diag_hbm.at[rows], diag.at[rows], weight_sem.at[2 * g + 1]),
        ))
        for copy in weights[-1]:
            copy.start()
        if g == 0:
            load("sens", sens_hbm, sens)

    def remote(source, target, send, recv, peer):
        copy = pltpu.make_async_remote_copy(
            src_ref=source, dst_ref=target, send_sem=send, recv_sem=recv, device_id=peer, device_id_type=MESH
        )
        copy.start()
        return copy

    def keep(s, i, value):
        local[s][i] = value
        if i < 4:
            edge[s][0, i + 2] = value
        if i >= B - 4:
            edge[s][1, i - (B - 4)] = value

    def send_halo(s):
        return (
            remote(local[s].at[pl.ds(B - 2, 2)], edge[s].at[0, pl.ds(0, 2)], halo_s.at[s, 0], halo_r.at[s, 0], right),
            remote(local[s].at[pl.ds(0, 2)], edge[s].at[1, pl.ds(4, 2)], halo_s.at[s, 1], halo_r.at[s, 1], left),
        )

    sent = []
    loads["psi0"].wait()
    loads["psi1"].wait()
    for i in (0, 1, B - 2, B - 1):
        keep(0, i, psi[i].astype(BF))
    loads["owner"].wait()
    owners = owner[...]
    slot, lane = iota((B, 128), 0), iota((B, 128), 1)
    high = (owners >> 6).astype(F32).astype(BF)
    low = (owners & 63).astype(F32).astype(BF)

    def owner_row(first):
        pick = jnp.where(slot == first + (lane & 7), 1.0, 0.0).astype(BF)
        spread = dot(high, pick) * 64.0 + dot(low, pick)
        return jnp.sum(jnp.where(slot == lane >> 3, spread, 0.0), axis=0, keepdims=True).astype(I32)

    tgt[0] = owner_row(8)
    near_owner = owner_row(0)

    pl.semaphore_wait(barrier, len(everyone))
    halo = send_halo(0)
    tgt_copies = [remote(tgt.at[0], tgt.at[k + 1], tgt_s.at[k], tgt_r.at[k], p) for k, p in enumerate(z_peers)]

    loads["psi"].wait()
    for i in range(2, B - 2):
        keep(0, i, psi[i].astype(BF))
    loads["nbr"].wait()
    loads["rhs"].wait()

    def block(s, i, read, first, count):
        nearby = [read(jnp.clip(nbr[k, i] - (h * B + first), 0, count - 1)) for k in range(NBR)]
        coupled = dot(jnp.concatenate(nearby, axis=1), couple[i].reshape(NBR * R, R))
        updated = (rhs[i] - coupled).astype(BF)
        return dot(updated, diag[i])

    def interior(s, i):
        return block(s, i, lambda p: local[s][p], 0, B)

    def boundary(s, i):
        side = 0 if i < 2 else 1
        return block(s, i, lambda p: edge[s][side, p], -2 if side == 0 else B - 4, 6)

    far, near = [], []

    def finish(i, value):
        adj[i] = value
        terms = dot(value.astype(BF), st[...])
        mine = iota((FN, 128), 1) >> 3 == i
        far.append(jnp.where(mine, terms[:, :128], 0.0))
        near.append(jnp.where(mine, terms[:, 128:], 0.0))

    outs = []

    def put(a, b):
        rows = pl.ds(a, b - a)
        outs.append(pltpu.make_async_copy(adj.at[rows], adj_hbm.at[rows], out_sem.at[len(outs)]))
        outs[-1].start()

    for s in range(SWEEPS):
        last = s == SWEEPS - 1
        for g, (a, b) in enumerate(GROUPS):
            if a == 0:
                if s == 0:
                    loads["sens"].wait()
                    wide = sens[...].astype(F32)
                    for q, first in enumerate((8, 0)):
                        part = wide[:, first:first + 8, :].reshape(128, R)
                        st[:, q * 128:(q + 1) * 128] = (-jnp.transpose(part)).astype(BF)
                    block_of = near_owner >> 4
                    group = jnp.where(block_of == h, 0, jnp.where(block_of == h - 1, 128, 256))
                    place = jnp.where(jnp.abs(block_of - h) <= 1, group + lane_of(near_owner), -1)
                    column = jnp.transpose(jnp.broadcast_to(place, (8, 128)).astype(F32))[:, :1].astype(I32)
                    ohn[...] = jnp.where(column == iota((128, 384), 1), 1.0, 0.0).astype(BF)
                if s == 1:
                    for copy in tgt_copies:
                        copy.wait_recv()
                    rows = jnp.concatenate([tgt[k] for k in range(NZ)], axis=0)
                    hull = rows >> 4
                    place = jnp.where(hull % NZ == z, (hull // (NY * NZ)) * 128 + lane_of(rows), -1)
                    if NZ < 8:
                        place = jnp.concatenate([place] * (8 // NZ), axis=0)
                    columns = jnp.transpose(place.astype(F32)).astype(I32)
                    for k in range(NZ):
                        oh[k * 128:(k + 1) * 128, :] = jnp.where(
                            columns[:, k:k + 1] == iota((128, NX * 128), 1), 1.0, 0.0
                        ).astype(BF)
                for copy in halo:
                    copy.wait_recv()
            if s == 0:
                for copy in weights[g]:
                    copy.wait()
            for i in range(a, b):
                value = boundary(s, i) if a == 0 or b == B else interior(s, i)
                if last:
                    finish(i, value)
                else:
                    keep(s + 1, i, value.astype(BF))
            if last and b == B - 2:
                put(2, B - 2)
        sent += halo
        if not last:
            halo = send_halo(s + 1)
    put(0, 2)
    put(B - 2, B)

    crecv[0] = sum(far).astype(BF)
    c_copies = [remote(crecv.at[0], crecv.at[k + 1], c_s.at[k], c_r.at[k], p) for k, p in enumerate(z_peers)]
    close = dot(sum(near).astype(BF), ohn[...])
    nsend[0] = close[:, 128:256]
    nsend[1] = close[:, 256:]
    n_copies = [remote(nsend.at[k], nrecv.at[k], n_s.at[k], n_r.at[k], p) for k, p in enumerate((left, right))]
    for copy in c_copies:
        copy.wait_recv()
    dense = dot(jnp.concatenate([crecv[k] for k in range(NZ)], axis=1), oh[...])

    for q in range(NX):
        dsend[q] = dense[:, q * 128:(q + 1) * 128]
    x_copies = [
        remote(dsend.at[(x + k + 1) % NX], xrecv.at[k], x_s.at[k], x_r.at[k], p) for k, p in enumerate(x_peers)
    ]
    for copy in n_copies:
        copy.wait_recv()
    total = close[:, :128] + nrecv[0] + nrecv[1] + dsend[x]
    for copy in x_copies:
        copy.wait_recv()
    for k in range(NX - 1):
        total = total + xrecv[k]

    stacked = jnp.concatenate([total if g == 0 else pltpu.roll(total, 128 - 32 * g, 1) for g in range(4)], axis=0)
    packed = jnp.transpose(stacked)
    for d in range(2 * NY):
        psend[d] = packed[2 * d:2 * d + 2, :]
    p_copies = [
        remote(
            psend.at[((y + k) % NY) * 2 + (core + e) % 2], precv.at[e * NY + k], p_s.at[m], p_r.at[m], yc_peers[m]
        )
        for m, (k, e) in enumerate(yc)
    ]
    own = psend[y * 2 + core]
    for copy in p_copies:
        copy.wait_recv()
    halves = []
    for e in range(2):
        half = own if e == 0 else precv[NY]
        for k in range(1, NY):
            half = half + precv[e * NY + k]
        halves.append(half)
    ordered = (jnp.where(core == 0, halves[0], halves[1]), jnp.where(core == 0, halves[1], halves[0]))
    row, lane = iota((8, 128), 0), iota((8, 128), 1)
    wide = [jnp.where(row < 4, half[0:1], half[1:2]) for half in ordered]
    result = jnp.zeros((8, 128), F32)
    for g in range(4):
        first = wide[0] if g == 0 else pltpu.roll(wide[0], 128 - 32 * g, 1)
        second = wide[1] if g == 1 else pltpu.roll(wide[1], (160 - 32 * g) % 128, 1)
        result = jnp.where((row & 3) == g, jnp.where(lane < FN, first, second), result)
    grad_ref[...] = result[:, :2 * FN]

    for copy in list(sent) + tgt_copies + c_copies + n_copies + x_copies + p_copies:
        copy.wait_send()
    for copy in outs:
        copy.wait()


def shards(adj_rhs, psi_init, couple, diag_inv, neighbours, sens, owner):
    vmem, dma = pltpu.VMEM, pltpu.SemaphoreType.DMA
    return pl.pallas_call(
        kernel,
        out_shape=(jax.ShapeDtypeStruct((B, FN, R), F32), jax.ShapeDtypeStruct((8, 2 * FN), F32)),
        in_specs=[pl.BlockSpec(memory_space=pl.ANY)] * 7,
        out_specs=(pl.BlockSpec(memory_space=pl.ANY), pl.BlockSpec(memory_space=pltpu.VMEM)),
        scratch_shapes=[
            vmem((B, FN, R), F32),
            vmem((B, FN, R), F32),
            vmem((B, NBR, R, R), BF),
            vmem((B, R, R), BF),
            pltpu.SMEM((NBR, B), I32),
            vmem((B, KLOC, R), BF),
            vmem((B, KLOC), I32),
            vmem((B, FN, R), F32),
            *[vmem((B, FN, R), BF)] * SWEEPS,
            *[vmem((2, 6, FN, R), BF)] * SWEEPS,
            vmem((R, 256), BF),
            vmem((NZ, 1, 128), I32),
            vmem((NZ * 128, NX * 128), BF),
            vmem((128, 384), BF),
            vmem((NZ, FN, 128), BF),
            vmem((2, FN, 128), F32),
            vmem((2, FN, 128), F32),
            vmem((NX, FN, 128), F32),
            vmem((NX - 1, FN, 128), F32),
            vmem((16, 2, 128), F32),
            vmem((2 * NY, 2, 128), F32),
            dma((7,)), dma((2 * len(GROUPS),)), dma((3,)),
            dma((SWEEPS, 2)), dma((SWEEPS, 2)),
            dma((NZ - 1,)), dma((NZ - 1,)), dma((NZ - 1,)), dma((NZ - 1,)),
            dma((2,)), dma((2,)),
            dma((NX - 1,)), dma((NX - 1,)),
            dma((2 * NY - 1,)), dma((2 * NY - 1,)),
        ],
        compiler_params=pltpu.CompilerParams(
            collective_id=0, has_side_effects=True, vmem_limit_bytes=63 * 2**20
        ),
        name="adjoint_gradient",
    )(adj_rhs, psi_init, couple, diag_inv, neighbours.T, sens, owner)


def solution(mesh):
    return jax.shard_map(
        shards,
        mesh=mesh,
        in_specs=(
            P("hull", "fn", None),
            P("hull", "fn", None),
            P("hull", None, None, None),
            P("hull", None, None),
            P("hull", None),
            P("hull", None, None),
            P("hull", None),
        ),
        out_specs=(P("hull", "fn", None), P(("hull", "fn"), None)),
        check_vma=False,
    )
```

```python
import functools

import jax
import jax.numpy as jnp
from jax import lax
from jax.experimental import pallas as pl
from jax.experimental.pallas import tpu as pltpu
from jax.sharding import PartitionSpec as P

MESH = pl.DeviceIdType.MESH
BF, F32, I32 = jnp.bfloat16, jnp.float32, jnp.int32
NX, NY, NZ = 4, 8, 8
B = 16
FN = 32
R = 128
NBR, KLOC, SWEEPS, REACH = 6, 16, 3, 2
GROUPS = ((2, 6), (6, 10), (10, 14), (0, 2), (14, 16))
INNER = tuple(range(2, B - 2))
OUTER = (0, 1, B - 2, B - 1)


def dot(a, b):
    return jnp.dot(a, b, preferred_element_type=F32)


def iota(shape, dim):
    return lax.broadcasted_iota(I32, shape, dim)


def kernel(
    rhs_hbm, psi_hbm, couple_hbm, diag_hbm, nbr_hbm, sens_hbm, owner_hbm,
    adj_hbm, grad_ref,
    rhs, psi, couple, diag, nbr, sens, owner, adj,
    local0, local1, local2, edge0, edge1, edge2, st, tgt, oh, ohn, crecv, nsend, nrecv, psend, precv,
    load_sem, weight_sem, out_sem, halo_s, halo_r, tgt_s, tgt_r, c_s, c_r, n_s, n_r, p_s, p_r, plane_sem,
):
    local, edge = (local0, local1, local2), (edge0, edge1, edge2)
    h = lax.axis_index("hull")
    core = lax.axis_index("fn")
    n_hull = NX * NY * NZ
    x, y, z = h // (NY * NZ), (h // NZ) % NY, h % NZ

    def device(i, j, k, c):
        return ((i * NY + j) * NZ + k, c)

    has_left, has_right = h > 0, h < n_hull - 1
    left, right = (jnp.maximum(h - 1, 0), core), (jnp.minimum(h + 1, n_hull - 1), core)
    z_steps = sorted(range(1, NZ), key=lambda k: -min(k, NZ - k))
    z_peers = [device(x, y, (z + k) % NZ, core) for k in z_steps]
    x_peers = [device((x + k) % NX, y, z, core) for k in range(1, NX)]
    plane = [(e, i, k) for e in range(2) for i in range(NX) for k in range(NY) if (e, i, k) != (0, 0, 0)]
    plane.sort(key=lambda t: (-min(t[1], NX - t[1]) - min(t[2], NY - t[2]), -t[0]))
    plane_peers = [device((x + i) % NX, (y + k) % NY, z, (core + e) % 2) for e, i, k in plane]
    yc_peers = [p for p, (e, i, k) in zip(plane_peers, plane) if i == 0]

    barrier = pltpu.get_barrier_semaphore()
    everyone = z_peers + x_peers + yc_peers
    for there, peer in ((has_right, right), (has_left, left)):
        @pl.when(there)
        def _():
            pl.semaphore_signal(barrier, inc=1, device_id=peer, device_id_type=MESH)
    for peer in everyone:
        pl.semaphore_signal(barrier, inc=1, device_id=peer, device_id_type=MESH)

    loads = {}

    def load(name, source, target):
        loads[name] = pltpu.make_async_copy(source, target, load_sem.at[len(loads)])
        loads[name].start()

    load("psi0", psi_hbm.at[pl.ds(0, 2)], psi.at[pl.ds(0, 2)])
    load("psi1", psi_hbm.at[pl.ds(B - 2, 2)], psi.at[pl.ds(B - 2, 2)])
    load("owner", owner_hbm, owner)
    load("psi", psi_hbm.at[pl.ds(2, B - 4)], psi.at[pl.ds(2, B - 4)])
    load("nbr", nbr_hbm, nbr)
    load("rhs", rhs_hbm, rhs)
    weights = []
    for g, (a, b) in enumerate(GROUPS):
        rows = pl.ds(a, b - a)
        weights.append((
            pltpu.make_async_copy(couple_hbm.at[rows], couple.at[rows], weight_sem.at[2 * g]),
            pltpu.make_async_copy(diag_hbm.at[rows], diag.at[rows], weight_sem.at[2 * g + 1]),
        ))
        for copy in weights[-1]:
            copy.start()
        if g == 0:
            load("sens", sens_hbm, sens)

    def remote(source, target, send, recv, peer):
        copy = pltpu.make_async_remote_copy(
            src_ref=source, dst_ref=target, send_sem=send, recv_sem=recv, device_id=peer, device_id_type=MESH
        )
        copy.start()
        return copy

    def keep(s, i, value):
        local[s][i] = value
        if i < 4:
            edge[s][0, i + 2] = value
        if i >= B - 4:
            edge[s][1, i - (B - 4)] = value

    class Pair:
        def __init__(self, sources, targets, send, recv):
            self.copies = [
                pltpu.make_async_remote_copy(
                    src_ref=sources[k], dst_ref=targets[k], send_sem=send[k], recv_sem=recv[k],
                    device_id=(right, left)[k], device_id_type=MESH,
                )
                for k in range(2)
            ]

            @pl.when(has_right)
            def _():
                self.copies[0].start()

            @pl.when(has_left)
            def _():
                self.copies[1].start()

        def wait_recv(self):
            @pl.when(has_left)
            def _():
                self.copies[0].wait_recv()

            @pl.when(has_right)
            def _():
                self.copies[1].wait_recv()

        def wait_send(self):
            @pl.when(has_right)
            def _():
                self.copies[0].wait_send()

            @pl.when(has_left)
            def _():
                self.copies[1].wait_send()

    def send_halo(s):
        return Pair(
            (local[s].at[pl.ds(B - 2, 2)], local[s].at[pl.ds(0, 2)]),
            (edge[s].at[0, pl.ds(0, 2)], edge[s].at[1, pl.ds(4, 2)]),
            (halo_s.at[s, 0], halo_s.at[s, 1]),
            (halo_r.at[s, 0], halo_r.at[s, 1]),
        )

    @pl.when(jnp.logical_not(has_left))
    def _():
        for ref in edge:
            ref[0, 0:2] = jnp.zeros((2, FN, R), BF)
        nrecv[0] = jnp.zeros((FN, 128), F32)

    @pl.when(jnp.logical_not(has_right))
    def _():
        for ref in edge:
            ref[1, 4:6] = jnp.zeros((2, FN, R), BF)
        nrecv[1] = jnp.zeros((FN, 128), F32)

    sent = []
    loads["psi0"].wait()
    loads["psi1"].wait()
    for i in (0, 1, B - 2, B - 1):
        keep(0, i, psi[i].astype(BF))
    loads["owner"].wait()
    owners = owner[...]
    slot, lane = iota((B, 128), 0), iota((B, 128), 1)
    high = (owners >> 6).astype(F32).astype(BF)
    low = (owners & 63).astype(F32).astype(BF)

    def owner_row(first):
        pick = jnp.where(slot == first + (lane & 7), 1.0, 0.0).astype(BF)
        spread = dot(high, pick) * 64.0 + dot(low, pick)
        return jnp.sum(jnp.where(slot == lane >> 3, spread, 0.0), axis=0, keepdims=True).astype(I32)

    tgt[0] = owner_row(8)
    near_owner = owner_row(0)

    pl.semaphore_wait(barrier, len(everyone) + has_right.astype(I32) + has_left.astype(I32))
    for peer in x_peers:
        pl.semaphore_signal(plane_sem, inc=1, device_id=peer, device_id_type=MESH)
    halo = send_halo(0)
    tgt_copies = [remote(tgt.at[0], tgt.at[k], tgt_s.at[k - 1], tgt_r.at[k - 1], p) for k, p in zip(z_steps, z_peers)]

    loads["psi"].wait()
    for i in range(2, B - 2):
        keep(0, i, psi[i].astype(BF))

    def blocks(s, rows, read):
        updated = []
        for i in rows:
            nearby = jnp.concatenate([read(i, nbr[k, i] - h * B) for k in range(NBR)], axis=1)
            updated.append((rhs[i] - dot(nearby, couple[i].reshape(NBR * R, R))).astype(BF))
        return [dot(u, diag[i]) for u, i in zip(updated, rows)]

    def interior(s):
        return blocks(s, INNER, lambda i, p: local[s][jnp.clip(p, 0, B - 1)])

    def boundary(s):
        def read(i, p):
            if i < 2:
                return edge[s][0, jnp.clip(p + 2, 0, 5)]
            return edge[s][1, jnp.clip(p - (B - 4), 0, 5)]

        return blocks(s, OUTER, read)

    outs = []

    def put(a, b):
        rows = pl.ds(a, b - a)
        outs.append(pltpu.make_async_copy(adj.at[rows], adj_hbm.at[rows], out_sem.at[len(outs)]))
        outs[-1].start()

    def contributions(rows, values):
        terms = dot(jnp.concatenate([v.astype(BF) for v in values], axis=0), st[...])
        column = iota((FN, 256), 1) % 128 >> 3
        return sum(jnp.where(column == i, terms[FN * n:FN * (n + 1), :], 0.0) for n, i in enumerate(rows))

    loads["nbr"].wait()
    loads["rhs"].wait()
    for group in weights:
        for copy in group:
            copy.wait()
    for i, value in zip(INNER, interior(0)):
        keep(1, i, value.astype(BF))
    loads["sens"].wait()
    wide = sens[...].astype(F32)
    for q, first in enumerate((8, 0)):
        part = wide[:, first:first + 8, :].reshape(128, R)
        st[:, q * 128:(q + 1) * 128] = (-jnp.transpose(part)).astype(BF)
    block_of = near_owner >> 4
    group = jnp.where(block_of == h, 0, jnp.where(block_of == h - 1, 128, 256))
    place = group + (near_owner & 3) * 32 + ((near_owner >> 3) & 1) * 2 + ((near_owner >> 2) & 1)
    place = jnp.where(jnp.abs(block_of - h) <= 1, place, -1)
    column = jnp.transpose(jnp.broadcast_to(place, (8, 128)).astype(F32))[:, :1].astype(I32)
    ohn[...] = jnp.where(column == iota((128, 384), 1), 1.0, 0.0).astype(BF)

    for s in range(SWEEPS):
        last = s == SWEEPS - 1
        halo.wait_recv()
        sent.append(halo)
        values = boundary(s)
        if last:
            break
        for i, value in zip(OUTER, values):
            keep(s + 1, i, value.astype(BF))
        halo = send_halo(s + 1)
        inner = interior(s + 1)
        if s + 1 < SWEEPS - 1:
            for i, value in zip(INNER, inner):
                keep(s + 2, i, value.astype(BF))
            for copy in tgt_copies:
                copy.wait_recv()
            rows = jnp.concatenate([tgt[k] for k in range(NZ)], axis=0)
            hull = rows >> 4
            place = (rows & 3) * 128 + (hull // NZ) * 4 + ((rows >> 3) & 1) * 2 + ((rows >> 2) & 1)
            place = jnp.where(hull % NZ == z, place, -1)
            if NZ < 8:
                place = jnp.concatenate([place] * (8 // NZ), axis=0)
            columns = jnp.transpose(place.astype(F32)).astype(I32)
            for k in range(NZ):
                oh[k * 128:(k + 1) * 128, :] = jnp.where(columns[:, k:k + 1] == iota((128, 512), 1), 1.0, 0.0).astype(BF)
        else:
            for i, value in zip(INNER, inner):
                adj[i] = value
            put(2, B - 2)
            terms = contributions(INNER, inner)
    terms = terms + contributions(OUTER, values)

    terms = terms.astype(BF)
    crecv[0] = terms[:, :128]
    c_copies = [remote(crecv.at[0], crecv.at[k], c_s.at[k - 1], c_r.at[k - 1], p) for k, p in zip(z_steps, z_peers)]
    close = dot(terms[:, 128:], ohn[...])
    nsend[0] = close[:, 256:]
    nsend[1] = close[:, 128:256]
    n_copies = Pair(*[(ref.at[0], ref.at[1]) for ref in (nsend, nrecv, n_s, n_r)])
    for i, value in zip(OUTER, values):
        adj[i] = value
    put(0, 2)
    put(B - 2, B)
    n_copies.wait_recv()
    close = close[:, :128] + nrecv[0] + nrecv[1]
    stacked = jnp.concatenate([close if g == 0 else pltpu.roll(close, 128 - 32 * g, 1) for g in range(4)], axis=0)
    close = jnp.transpose(stacked)[:4, :]
    pl.semaphore_wait(plane_sem, NX - 1)
    for copy in c_copies:
        copy.wait_recv()
    dense = dot(jnp.concatenate([crecv[k] for k in range(NZ)], axis=1), oh[...])

    packed = jnp.transpose(jnp.concatenate([dense[:, g * 128:(g + 1) * 128] for g in range(4)], axis=0))
    for d in range(2 * NX * NY):
        psend[d] = packed[2 * d:2 * d + 2, :]
    mine = (x * NY + y) * 2
    psend[mine] += close[0:2, :]
    psend[mine + 1] += close[2:4, :]
    p_copies = [
        remote(
            psend.at[(((x + i) % NX) * NY + (y + k) % NY) * 2 + (core + e) % 2],
            precv.at[(e * NX + i) * NY + k], p_s.at[n], p_r.at[n], plane_peers[n],
        )
        for n, (e, i, k) in enumerate(plane)
    ]
    own = psend[mine + core]
    for copy in p_copies:
        copy.wait_recv()
    half = NX * NY
    halves = [own + jnp.sum(precv[1:half], axis=0), jnp.sum(precv[half:2 * half], axis=0)]
    ordered = (jnp.where(core == 0, halves[0], halves[1]), jnp.where(core == 0, halves[1], halves[0]))
    row, lane = iota((8, 128), 0), iota((8, 128), 1)
    wide = [jnp.where(row < 4, half[0:1], half[1:2]) for half in ordered]
    result = jnp.zeros((8, 128), F32)
    for g in range(4):
        first = wide[0] if g == 0 else pltpu.roll(wide[0], 128 - 32 * g, 1)
        second = wide[1] if g == 1 else pltpu.roll(wide[1], (160 - 32 * g) % 128, 1)
        result = jnp.where((row & 3) == g, jnp.where(lane < FN, first, second), result)
    grad_ref[...] = result[:, :2 * FN]

    for copy in sent + tgt_copies + c_copies + [n_copies] + p_copies:
        copy.wait_send()
    for copy in outs:
        copy.wait()


def emit(adj_in, grad_in, adj_out, grad_out, sem):
    copies = [
        pltpu.make_async_copy(adj_in, adj_out, sem.at[0]),
        pltpu.make_async_copy(grad_in, grad_out, sem.at[1]),
    ]
    for copy in copies:
        copy.start()
    for copy in copies:
        copy.wait()


def shards(adj_rhs, psi_init, couple, diag_inv, neighbours, sens, owner):
    vmem, dma = pltpu.VMEM, pltpu.SemaphoreType.DMA
    pinned = (pltpu.VMEM((B, FN, R), F32), pltpu.VMEM((8, 2 * FN), F32))
    shapes = (jax.ShapeDtypeStruct((B, FN, R), F32), jax.ShapeDtypeStruct((8, 2 * FN), F32))
    results = pl.pallas_call(
        kernel,
        out_shape=pinned,
        in_specs=[pl.BlockSpec(memory_space=pltpu.HBM)] * 7,
        out_specs=(pl.BlockSpec(memory_space=pl.ANY), pl.BlockSpec(memory_space=pltpu.VMEM)),
        scratch_shapes=[
            vmem((B, FN, R), F32),
            vmem((B, FN, R), F32),
            vmem((B, NBR, R, R), BF),
            vmem((B, R, R), BF),
            pltpu.SMEM((NBR, B), I32),
            vmem((B, KLOC, R), BF),
            vmem((B, KLOC), I32),
            vmem((B, FN, R), F32),
            *[vmem((B, FN, R), BF)] * SWEEPS,
            *[vmem((2, 6, FN, R), BF)] * SWEEPS,
            vmem((R, 256), BF),
            vmem((NZ, 1, 128), I32),
            vmem((NZ * 128, 512), BF),
            vmem((128, 384), BF),
            vmem((NZ, FN, 128), BF),
            vmem((2, FN, 128), F32),
            vmem((2, FN, 128), F32),
            vmem((64, 2, 128), F32),
            vmem((2 * NX * NY, 2, 128), F32),
            dma((7,)), dma((2 * len(GROUPS),)), dma((3,)),
            dma((SWEEPS, 2)), dma((SWEEPS, 2)),
            dma((NZ - 1,)), dma((NZ - 1,)), dma((NZ - 1,)), dma((NZ - 1,)),
            dma((2,)), dma((2,)),
            dma((2 * NX * NY - 1,)), dma((2 * NX * NY - 1,)),
            pltpu.SemaphoreType.REGULAR,
        ],
        compiler_params=pltpu.CompilerParams(
            collective_id=0, has_side_effects=True, vmem_limit_bytes=62 * 2**20
        ),
        name="adjoint_gradient",
    )(adj_rhs, psi_init, couple, diag_inv, neighbours.T, sens, owner)
    return pl.pallas_call(
        emit,
        out_shape=shapes,
        in_specs=[pl.BlockSpec(memory_space=pl.ANY)] * 2,
        out_specs=(pl.BlockSpec(memory_space=pl.ANY),) * 2,
        scratch_shapes=[dma((2,))],
        compiler_params=pltpu.CompilerParams(vmem_limit_bytes=24 * 2**20),
        name="emit",
    )(*results)


def solution(mesh):
    return jax.shard_map(
        shards,
        mesh=mesh,
        in_specs=(
            P("hull", "fn", None),
            P("hull", "fn", None),
            P("hull", None, None, None),
            P("hull", None, None),
            P("hull", None),
            P("hull", None, None),
            P("hull", None),
        ),
        out_specs=(P("hull", "fn", None), P(("hull", "fn"), None)),
        check_vma=False,
    )
```

```python
import functools

import jax
import jax.numpy as jnp
from jax import lax
from jax.experimental import pallas as pl
from jax.experimental.pallas import tpu as pltpu
from jax.sharding import PartitionSpec as P

MESH = pl.DeviceIdType.MESH
BF, F32, I32 = jnp.bfloat16, jnp.float32, jnp.int32
NX, NY, NZ = 4, 8, 8
B = 16
FN = 32
R = 128
NBR, KLOC, SWEEPS, REACH = 6, 16, 3, 2
GROUPS = ((2, 6), (6, 10), (10, 14), (0, 2), (14, 16))
INNER = tuple(range(2, B - 2))
MIDDLE = tuple(range(4, B - 4))
BETWEEN = (2, 3, B - 4, B - 3)
OUTER = (0, 1, B - 2, B - 1)


def dot(a, b):
    return jnp.dot(a, b, preferred_element_type=F32)


def dot_t(a, b):
    return lax.dot_general(a, b, (((1,), (1,)), ((), ())), preferred_element_type=F32)


def iota(shape, dim):
    return lax.broadcasted_iota(I32, shape, dim)


def kernel(
    rhs_hbm, psi_hbm, couple_hbm, diag_hbm, nbr_hbm, sens_hbm, owner_hbm,
    adj_hbm, grad_ref,
    rhs, psi, couple, diag, nbr, sens, owner, adj,
    local0, local1, local2, edge0, edge1, edge2, part, st, osend, orecv, vsend, vrecv, vt,
    tgt, oh, ohn, crecv, nsend, nrecv, psend, precv,
    load_sem, weight_sem, out_sem, halo_s, halo_r, o_s, o_r, v_s, v_r, tgt_s, tgt_r, c_s, c_r, n_s, n_r, p_s, p_r,
    known1, known2, known3,
):
    local, edge = (local0, local1, local2), (edge0, edge1, edge2)
    h = lax.axis_index("hull")
    core = lax.axis_index("fn")
    n_hull = NX * NY * NZ
    x, y, z = h // (NY * NZ), (h // NZ) % NY, h % NZ

    def device(i, j, k, c):
        return ((i * NY + j) * NZ + k, c)

    has_left, has_right = h > 0, h < n_hull - 1
    left, right = (jnp.maximum(h - 1, 0), core), (jnp.minimum(h + 1, n_hull - 1), core)
    z_steps = sorted(range(1, NZ), key=lambda k: -min(k, NZ - k))
    z_peers = [device(x, y, (z + k) % NZ, core) for k in z_steps]
    x_peers = [device((x + k) % NX, y, z, core) for k in range(1, NX)]
    plane = [(e, i, k) for e in range(2) for i in range(NX) for k in range(NY) if (e, i, k) != (0, 0, 0)]
    plane.sort(key=lambda t: (-min(t[1], NX - t[1]) - min(t[2], NY - t[2]), -t[0]))
    plane_peers = [device((x + i) % NX, (y + k) % NY, z, (core + e) % 2) for e, i, k in plane]
    twin = [(h, 1 - core)]

    def within(n, far):
        return [k for k in range(1, n) if min(k, n - k) in far]

    def along(far):
        steps_z = [device(x, y, (z + k) % NZ, core) for k in within(NZ, far)]
        return steps_z + [device(x, (y + k) % NY, z, core) for k in within(NY, far)]

    def tell(semaphore, peers):
        for peer in peers:
            pl.semaphore_signal(semaphore, inc=1, device_id=peer, device_id_type=MESH)

    barrier = pltpu.get_barrier_semaphore()
    for there, peer in ((has_right, right), (has_left, left)):
        @pl.when(there)
        def _():
            tell(barrier, [peer])
    close_peers = along((1, 2)) + x_peers + twin
    tell(barrier, close_peers)
    round1, round2, round3 = along((2,)) + twin, x_peers + twin, x_peers

    loads = {}

    def load(name, source, target):
        loads[name] = pltpu.make_async_copy(source, target, load_sem.at[len(loads)])
        loads[name].start()

    load("psi0", psi_hbm.at[pl.ds(0, 2)], psi.at[pl.ds(0, 2)])
    load("psi1", psi_hbm.at[pl.ds(B - 2, 2)], psi.at[pl.ds(B - 2, 2)])
    load("owner", owner_hbm, owner)
    load("psi", psi_hbm.at[pl.ds(2, B - 4)], psi.at[pl.ds(2, B - 4)])
    load("nbr", nbr_hbm, nbr)
    load("rhs", rhs_hbm, rhs)
    weights = []
    for g, (a, b) in enumerate(GROUPS):
        rows = pl.ds(a, b - a)
        weights.append((
            pltpu.make_async_copy(couple_hbm.at[rows], couple.at[rows], weight_sem.at[2 * g]),
            pltpu.make_async_copy(diag_hbm.at[rows], diag.at[rows], weight_sem.at[2 * g + 1]),
        ))
        for copy in weights[-1]:
            copy.start()
        if g == 0:
            load("sens", sens_hbm, sens)

    def remote(source, target, send, recv, peer):
        copy = pltpu.make_async_remote_copy(
            src_ref=source, dst_ref=target, send_sem=send, recv_sem=recv, device_id=peer, device_id_type=MESH
        )
        copy.start()
        return copy

    def keep(s, i, value):
        local[s][i] = value
        if i < 4:
            edge[s][0, i + 2] = value
            if s == SWEEPS - 1:
                part[0, i + 2] = value
        if i >= B - 4:
            edge[s][1, i - (B - 4)] = value
            if s == SWEEPS - 1:
                part[1, i - (B - 4)] = value

    class Pair:
        def __init__(self, sources, targets, send, recv):
            self.copies = [
                pltpu.make_async_remote_copy(
                    src_ref=sources[k], dst_ref=targets[k], send_sem=send[k], recv_sem=recv[k],
                    device_id=(right, left)[k], device_id_type=MESH,
                )
                for k in range(2)
            ]

            @pl.when(has_right)
            def _():
                self.copies[0].start()

            @pl.when(has_left)
            def _():
                self.copies[1].start()

        def wait_recv(self):
            @pl.when(has_left)
            def _():
                self.copies[0].wait_recv()

            @pl.when(has_right)
            def _():
                self.copies[1].wait_recv()

        def wait_send(self):
            @pl.when(has_right)
            def _():
                self.copies[0].wait_send()

            @pl.when(has_left)
            def _():
                self.copies[1].wait_send()

    def send_halo(s):
        return Pair(
            (local[s].at[pl.ds(B - 2, 2)], local[s].at[pl.ds(0, 2)]),
            (edge[s].at[0, pl.ds(0, 2)], edge[s].at[1, pl.ds(4, 2)]),
            (halo_s.at[s, 0], halo_s.at[s, 1]),
            (halo_r.at[s, 0], halo_r.at[s, 1]),
        )

    @pl.when(jnp.logical_not(has_left))
    def _():
        for ref in edge:
            ref[0, 0:2] = jnp.zeros((2, FN, R), BF)
        nrecv[0] = jnp.zeros((FN, 128), F32)
        orecv[0] = jnp.full((1, 128), -1, I32)
        vrecv[0] = jnp.zeros((32, 256), BF)

    @pl.when(jnp.logical_not(has_right))
    def _():
        for ref in edge:
            ref[1, 4:6] = jnp.zeros((2, FN, R), BF)
        nrecv[1] = jnp.zeros((FN, 128), F32)
        orecv[1] = jnp.full((1, 128), -1, I32)
        vrecv[1] = jnp.zeros((32, 256), BF)

    part[0, 0:2] = jnp.zeros((2, FN, R), BF)
    part[1, 4:6] = jnp.zeros((2, FN, R), BF)

    loads["psi0"].wait()
    loads["psi1"].wait()
    for i in (0, 1, B - 2, B - 1):
        keep(0, i, psi[i].astype(BF))
    loads["owner"].wait()
    owners = owner[...]
    slot, lane = iota((B, 128), 0), iota((B, 128), 1)
    high = (owners >> 6).astype(F32).astype(BF)
    low = (owners & 63).astype(F32).astype(BF)

    def owner_row(block_row, block_slot):
        pick = jnp.where(slot == block_slot, 1.0, 0.0).astype(BF)
        spread = dot(high, pick) * 64.0 + dot(low, pick)
        return jnp.sum(jnp.where(slot == block_row, spread, 0.0), axis=0, keepdims=True).astype(I32)

    far_owner = owner_row(lane >> 3, 8 + (lane & 7))
    near_owner = owner_row(lane >> 3, lane & 7)
    osend[...] = owner_row(jnp.where((lane & 63) < 32, B - 2, 0) + ((lane >> 4) & 1), lane & 15)

    pl.semaphore_wait(barrier, len(close_peers) + has_right.astype(I32) + has_left.astype(I32))
    halo = send_halo(0)
    o_copies = Pair((osend, osend), (orecv.at[0], orecv.at[1]), (o_s.at[0], o_s.at[1]), (o_r.at[0], o_r.at[1]))
    tell(known1, round1)

    loads["psi"].wait()
    for i in range(2, B - 2):
        keep(0, i, psi[i].astype(BF))

    def blocks(s, rows, read):
        updated = []
        for i in rows:
            nearby = jnp.concatenate([read(i, nbr[k, i] - h * B) for k in range(NBR)], axis=1)
            updated.append((rhs[i] - dot(nearby, couple[i].reshape(NBR * R, R))).astype(BF))
        return [dot(u, diag[i]) for u, i in zip(updated, rows)]

    def from_local(s, i, p):
        return local[s][jnp.clip(p, 0, B - 1)]

    def interior(s, rows):
        return blocks(s, rows, lambda i, p: from_local(s, i, p))

    def from_edge(ref, i, p):
        return ref[0, jnp.clip(p + 2, 0, 5)] if i < 2 else ref[1, jnp.clip(p - (B - 4), 0, 5)]

    def boundary(s):
        return blocks(s, OUTER, lambda i, p: from_edge(edge[s], i, p))

    outs = []

    def put(a, b):
        rows = pl.ds(a, b - a)
        outs.append(pltpu.make_async_copy(adj.at[rows], adj_hbm.at[rows], out_sem.at[len(outs)]))
        outs[-1].start()

    def contributions(rows, values):
        terms = dot(jnp.concatenate([v.astype(BF) for v in values], axis=0), st[...])
        column = iota((FN, 256), 1) % 128 >> 3
        return sum(jnp.where(column == i, terms[FN * n:FN * (n + 1), :], 0.0) for n, i in enumerate(rows))

    loads["nbr"].wait()
    loads["rhs"].wait()
    for group in weights:
        for copy in group:
            copy.wait()
    for i, value in zip(INNER, interior(0, INNER)):
        keep(1, i, value.astype(BF))
    loads["sens"].wait()
    wide = sens[...].astype(F32)
    for q, first in enumerate((8, 0)):
        chunk = wide[:, first:first + 8, :].reshape(128, R)
        st[:, q * 128:(q + 1) * 128] = (-jnp.transpose(chunk)).astype(BF)
    block_of = near_owner >> 4
    group = jnp.where(block_of == h, 0, jnp.where(block_of == h - 1, 128, 256))
    place = group + (near_owner & 3) * 32 + ((near_owner >> 3) & 1) * 2 + ((near_owner >> 2) & 1)
    place = jnp.where(jnp.abs(block_of - h) <= 1, place, -1)
    column = jnp.transpose(jnp.broadcast_to(place, (8, 128)).astype(F32))[:, :1].astype(I32)
    ohn[...] = jnp.where(column == iota((128, 384), 1), 1.0, 0.0).astype(BF)

    for side, (rows, others) in enumerate((((B - 2, B - 1), (B, B + 1)), ((0, 1), (-2, -1)))):
        for n, i in enumerate(rows):
            shape = dot_t(sens[i], diag[i]).astype(BF)
            slots = dot_t(shape, couple[i].reshape(NBR * R, R))
            for m, j in enumerate(others):
                vsend[side, n * KLOC:(n + 1) * KLOC, m * R:(m + 1) * R] = sum(
                    jnp.where(nbr[k, i] - h * B == j, slots[:, k * R:(k + 1) * R], 0.0) for k in range(NBR)
                ).astype(BF)
    v_copies = Pair(*[(ref.at[0], ref.at[1]) for ref in (vsend, vrecv, v_s, v_r)])

    pl.semaphore_wait(known1, len(round1))
    tell(known2, round2)
    o_copies.wait_recv()
    lane = iota((1, 128), 1)
    tgt[0] = jnp.concatenate([far_owner, jnp.where((lane & 63) < 32, orecv[0], orecv[1])], axis=0)
    tgt_copies = [
        remote(tgt.at[0], tgt.at[k], tgt_s.at[k - 1], tgt_r.at[k - 1], p) for k, p in zip(z_steps, z_peers)
    ]

    halo.wait_recv()
    sent = [halo, o_copies, v_copies]
    for i, value in zip(OUTER, boundary(0)):
        keep(1, i, value.astype(BF))
    halo = send_halo(1)
    for i, value in zip(INNER, interior(1, INNER)):
        keep(2, i, value.astype(BF))
    values = interior(2, MIDDLE)
    for i, value in zip(MIDDLE, values):
        adj[i] = value
    put(MIDDLE[0], MIDDLE[-1] + 1)
    terms = contributions(MIDDLE, values)
    pl.semaphore_wait(known2, len(round2))
    tell(known3, round3)
    v_copies.wait_recv()
    zero = jnp.zeros((32, 256), F32)
    vt[...] = jnp.transpose(
        jnp.concatenate(
            [
                jnp.concatenate([vrecv[0].astype(F32), zero], axis=1),
                jnp.concatenate([zero, vrecv[1].astype(F32)], axis=1),
                jnp.zeros((64, 512), F32),
            ],
            axis=0,
        )
    ).astype(BF)

    halo.wait_recv()
    sent.append(halo)
    for i, value in zip(OUTER, boundary(1)):
        keep(2, i, value.astype(BF))
    halo = send_halo(2)
    sent.append(halo)

    rows = BETWEEN + OUTER
    values = blocks(2, rows, lambda i, p: from_edge(part, i, p) if i in OUTER else from_local(2, i, p))
    terms = (terms + contributions(rows, values)).astype(BF)
    beyond = dot(jnp.concatenate([local[2][i] for i in OUTER], axis=1), vt[...])
    lane = iota((16, 128), 1)
    crecv[0, 0:FN] = terms[:, :128]
    crecv[0, FN:48] = jnp.where(lane < 64, beyond[:16], pltpu.roll(beyond[16:], 64, 1)).astype(BF)

    c_copies = [remote(crecv.at[0], crecv.at[k], c_s.at[k - 1], c_r.at[k - 1], p) for k, p in zip(z_steps, z_peers)]
    close = dot(terms[:, 128:], ohn[...])
    nsend[0] = close[:, 256:]
    nsend[1] = close[:, 128:256]
    n_copies = Pair(*[(ref.at[0], ref.at[1]) for ref in (nsend, nrecv, n_s, n_r)])
    for i, value in zip(BETWEEN, values):
        adj[i] = value
    put(2, 4)
    put(B - 4, B - 2)
    for copy in tgt_copies:
        copy.wait_recv()
    for n in range(2):
        rows = jnp.concatenate([tgt[k, n:n + 1] for k in range(NZ)], axis=0)
        hull = rows >> 4
        place = (rows & 3) * 128 + (hull // NZ) * 4 + ((rows >> 3) & 1) * 2 + ((rows >> 2) & 1)
        place = jnp.where((hull % NZ == z) & (rows >= 0), place, -1)
        if NZ < 8:
            place = jnp.concatenate([place] * (8 // NZ), axis=0)
        columns = jnp.transpose(place.astype(F32)).astype(I32)
        for k in range(NZ):
            oh[(n * NZ + k) * 128:(n * NZ + k + 1) * 128, :] = jnp.where(
                columns[:, k:k + 1] == iota((128, 512), 1), 1.0, 0.0
            ).astype(BF)
    n_copies.wait_recv()
    close = close[:, :128] + nrecv[0] + nrecv[1]
    stacked = jnp.concatenate([close if g == 0 else pltpu.roll(close, 128 - 32 * g, 1) for g in range(4)], axis=0)
    close = jnp.transpose(stacked)[:4, :]
    pl.semaphore_wait(known3, len(round3))
    for copy in c_copies:
        copy.wait_recv()
    lane = iota((16, 128), 1)
    extra = []
    for k in range(NZ):
        both = crecv[k, FN:48].astype(F32)
        halves = [jnp.where(lane < 64, both, 0.0), jnp.where(lane < 64, 0.0, both)]
        extra.append(jnp.concatenate(halves, axis=0).astype(BF))
    dense = dot(jnp.concatenate([crecv[k, 0:FN] for k in range(NZ)] + extra, axis=1), oh[...])

    packed = jnp.transpose(jnp.concatenate([dense[:, g * 128:(g + 1) * 128] for g in range(4)], axis=0))
    for d in range(2 * NX * NY):
        psend[d] = packed[2 * d:2 * d + 2, :]
    mine = (x * NY + y) * 2
    psend[mine] += close[0:2, :]
    psend[mine + 1] += close[2:4, :]
    p_copies = [
        remote(
            psend.at[(((x + i) % NX) * NY + (y + k) % NY) * 2 + (core + e) % 2],
            precv.at[(e * NX + i) * NY + k], p_s.at[n], p_r.at[n], plane_peers[n],
        )
        for n, (e, i, k) in enumerate(plane)
    ]
    own = psend[mine + core]
    halo.wait_recv()
    for i, value in zip(OUTER, boundary(2)):
        adj[i] = value
    put(0, 2)
    put(B - 2, B)
    for copy in p_copies:
        copy.wait_recv()
    half = NX * NY
    halves = [own + jnp.sum(precv[1:half], axis=0), jnp.sum(precv[half:2 * half], axis=0)]
    ordered = (jnp.where(core == 0, halves[0], halves[1]), jnp.where(core == 0, halves[1], halves[0]))
    row, lane = iota((8, 128), 0), iota((8, 128), 1)
    wide = [jnp.where(row < 4, half[0:1], half[1:2]) for half in ordered]
    result = jnp.zeros((8, 128), F32)
    for g in range(4):
        first = wide[0] if g == 0 else pltpu.roll(wide[0], 128 - 32 * g, 1)
        second = wide[1] if g == 1 else pltpu.roll(wide[1], (160 - 32 * g) % 128, 1)
        result = jnp.where((row & 3) == g, jnp.where(lane < FN, first, second), result)
    grad_ref[...] = result[:, :2 * FN]

    for copy in sent + tgt_copies + c_copies + [n_copies] + p_copies:
        copy.wait_send()
    for copy in outs:
        copy.wait()


def emit(adj_in, grad_in, adj_out, grad_out, sem):
    copies = [
        pltpu.make_async_copy(adj_in, adj_out, sem.at[0]),
        pltpu.make_async_copy(grad_in, grad_out, sem.at[1]),
    ]
    for copy in copies:
        copy.start()
    for copy in copies:
        copy.wait()


def shards(adj_rhs, psi_init, couple, diag_inv, neighbours, sens, owner):
    vmem, dma = pltpu.VMEM, pltpu.SemaphoreType.DMA
    pinned = (pltpu.VMEM((B, FN, R), F32), pltpu.VMEM((8, 2 * FN), F32))
    shapes = (jax.ShapeDtypeStruct((B, FN, R), F32), jax.ShapeDtypeStruct((8, 2 * FN), F32))
    results = pl.pallas_call(
        kernel,
        out_shape=pinned,
        in_specs=[pl.BlockSpec(memory_space=pltpu.HBM)] * 7,
        out_specs=(pl.BlockSpec(memory_space=pl.ANY), pl.BlockSpec(memory_space=pltpu.VMEM)),
        scratch_shapes=[
            vmem((B, FN, R), F32),
            vmem((B, FN, R), F32),
            vmem((B, NBR, R, R), BF),
            vmem((B, R, R), BF),
            pltpu.SMEM((NBR, B), I32),
            vmem((B, KLOC, R), BF),
            vmem((B, KLOC), I32),
            vmem((B, FN, R), F32),
            *[vmem((B, FN, R), BF)] * SWEEPS,
            *[vmem((2, 6, FN, R), BF)] * SWEEPS,
            vmem((2, 6, FN, R), BF),
            vmem((R, 256), BF),
            vmem((1, 128), I32),
            vmem((2, 1, 128), I32),
            vmem((2, 32, 256), BF),
            vmem((2, 32, 256), BF),
            vmem((512, 128), BF),
            vmem((NZ, 2, 128), I32),
            vmem((2 * NZ * 128, 512), BF),
            vmem((128, 384), BF),
            vmem((NZ, 48, 128), BF),
            vmem((2, FN, 128), F32),
            vmem((2, FN, 128), F32),
            vmem((64, 2, 128), F32),
            vmem((2 * NX * NY, 2, 128), F32),
            dma((7,)), dma((2 * len(GROUPS),)), dma((5,)),
            dma((SWEEPS, 2)), dma((SWEEPS, 2)),
            dma((2,)), dma((2,)), dma((2,)), dma((2,)),
            dma((NZ - 1,)), dma((NZ - 1,)), dma((NZ - 1,)), dma((NZ - 1,)),
            dma((2,)), dma((2,)),
            dma((2 * NX * NY - 1,)), dma((2 * NX * NY - 1,)),
            *[pltpu.SemaphoreType.REGULAR] * 3,
        ],
        compiler_params=pltpu.CompilerParams(
            collective_id=0, has_side_effects=True, vmem_limit_bytes=62 * 2**20
        ),
        name="adjoint_gradient",
    )(adj_rhs, psi_init, couple, diag_inv, neighbours.T, sens, owner)
    return pl.pallas_call(
        emit,
        out_shape=shapes,
        in_specs=[pl.BlockSpec(memory_space=pl.ANY)] * 2,
        out_specs=(pl.BlockSpec(memory_space=pl.ANY),) * 2,
        scratch_shapes=[dma((2,))],
        compiler_params=pltpu.CompilerParams(vmem_limit_bytes=24 * 2**20),
        name="emit",
    )(*results)


def solution(mesh):
    return jax.shard_map(
        shards,
        mesh=mesh,
        in_specs=(
            P("hull", "fn", None),
            P("hull", "fn", None),
            P("hull", None, None, None),
            P("hull", None, None),
            P("hull", None),
            P("hull", None, None),
            P("hull", None),
        ),
        out_specs=(P("hull", "fn", None), P(("hull", "fn"), None)),
        check_vma=False,
    )
```

```python
import functools

import jax
import jax.numpy as jnp
from jax import lax
from jax.experimental import pallas as pl
from jax.experimental.pallas import tpu as pltpu
from jax.sharding import PartitionSpec as P

MESH = pl.DeviceIdType.MESH
BF, F32, I32 = jnp.bfloat16, jnp.float32, jnp.int32
NX, NY, NZ = 4, 8, 8
B = 16
FN = 32
R = 128
NBR, KLOC, SWEEPS, REACH = 6, 16, 3, 2
GROUPS = ((2, 6), (6, 10), (10, 14), (0, 2), (14, 16))
INNER = tuple(range(2, B - 2))
MIDDLE = tuple(range(4, B - 4))
BETWEEN = (2, 3, B - 4, B - 3)
OUTER = (0, 1, B - 2, B - 1)


def dot(a, b):
    return jnp.dot(a, b, preferred_element_type=F32)


def dot_t(a, b):
    return lax.dot_general(a, b, (((1,), (1,)), ((), ())), preferred_element_type=F32)


def iota(shape, dim):
    return lax.broadcasted_iota(I32, shape, dim)


def kernel(
    rhs_hbm, psi_hbm, couple_hbm, diag_hbm, nbr_hbm, sens_hbm, owner_hbm,
    adj_hbm, grad_ref,
    rhs, psi, couple, diag, nbr, sens, owner, adj,
    local0, local1, local2, edge0, edge1, edge2, part, st, osend, orecv, vsend, vrecv, vt,
    tgt, oh, ohn, crecv, nsend, nrecv, psend, precv,
    load_sem, weight_sem, out_sem, halo_s, halo_r, o_s, o_r, v_s, v_r, tgt_s, tgt_r, c_s, c_r, n_s, n_r, p_s, p_r,
    known1, known2, known3,
):
    local, edge = (local0, local1, local2), (edge0, edge1, edge2)
    h = lax.axis_index("hull")
    core = lax.axis_index("fn")
    n_hull = NX * NY * NZ
    x, y, z = h // (NY * NZ), (h // NZ) % NY, h % NZ

    def device(i, j, k, c):
        return ((i * NY + j) * NZ + k, c)

    has_left, has_right = h > 0, h < n_hull - 1
    left, right = (jnp.maximum(h - 1, 0), core), (jnp.minimum(h + 1, n_hull - 1), core)
    z_steps = sorted(range(1, NZ), key=lambda k: -min(k, NZ - k))
    z_peers = [device(x, y, (z + k) % NZ, core) for k in z_steps]
    x_peers = [device((x + k) % NX, y, z, core) for k in range(1, NX)]
    plane = [(e, i, k) for e in range(2) for i in range(NX) for k in range(NY) if (e, i, k) != (0, 0, 0)]
    plane.sort(key=lambda t: (-min(t[1], NX - t[1]) - min(t[2], NY - t[2]), -t[0]))
    plane_peers = [device((x + i) % NX, (y + k) % NY, z, (core + e) % 2) for e, i, k in plane]
    twin = [(h, 1 - core)]

    def within(n, far):
        return [k for k in range(1, n) if min(k, n - k) in far]

    def along(far):
        steps_z = [device(x, y, (z + k) % NZ, core) for k in within(NZ, far)]
        return steps_z + [device(x, (y + k) % NY, z, core) for k in within(NY, far)]

    def tell(semaphore, peers):
        for peer in peers:
            pl.semaphore_signal(semaphore, inc=1, device_id=peer, device_id_type=MESH)

    barrier = pltpu.get_barrier_semaphore()
    for there, peer in ((has_right, right), (has_left, left)):
        @pl.when(there)
        def _():
            tell(barrier, [peer])
    close_peers = along((1, 2)) + x_peers + twin
    tell(barrier, close_peers)
    round1, round2, round3 = along((2,)) + twin, x_peers + twin, x_peers

    loads = {}

    def load(name, source, target):
        loads[name] = pltpu.make_async_copy(source, target, load_sem.at[len(loads)])
        loads[name].start()

    load("psi0", psi_hbm.at[pl.ds(0, 2)], psi.at[pl.ds(0, 2)])
    load("psi1", psi_hbm.at[pl.ds(B - 2, 2)], psi.at[pl.ds(B - 2, 2)])
    load("owner", owner_hbm, owner)
    load("psi", psi_hbm.at[pl.ds(2, B - 4)], psi.at[pl.ds(2, B - 4)])
    load("nbr", nbr_hbm, nbr)
    load("rhs", rhs_hbm, rhs)
    weights = []
    for g, (a, b) in enumerate(GROUPS):
        rows = pl.ds(a, b - a)
        weights.append((
            pltpu.make_async_copy(couple_hbm.at[rows], couple.at[rows], weight_sem.at[2 * g]),
            pltpu.make_async_copy(diag_hbm.at[rows], diag.at[rows], weight_sem.at[2 * g + 1]),
        ))
        for copy in weights[-1]:
            copy.start()
        if g == 0:
            load("sens", sens_hbm, sens)

    def remote(source, target, send, recv, peer):
        copy = pltpu.make_async_remote_copy(
            src_ref=source, dst_ref=target, send_sem=send, recv_sem=recv, device_id=peer, device_id_type=MESH
        )
        copy.start()
        return copy

    def keep(s, i, value):
        local[s][i] = value
        if i < 4:
            edge[s][0, i + 2] = value
            if s == SWEEPS - 1:
                part[0, i + 2] = value
        if i >= B - 4:
            edge[s][1, i - (B - 4)] = value
            if s == SWEEPS - 1:
                part[1, i - (B - 4)] = value

    class Pair:
        def __init__(self, sources, targets, send, recv):
            self.copies = [
                pltpu.make_async_remote_copy(
                    src_ref=sources[k], dst_ref=targets[k], send_sem=send[k], recv_sem=recv[k],
                    device_id=(right, left)[k], device_id_type=MESH,
                )
                for k in range(2)
            ]

            @pl.when(has_right)
            def _():
                self.copies[0].start()

            @pl.when(has_left)
            def _():
                self.copies[1].start()

        def wait_recv(self):
            @pl.when(has_left)
            def _():
                self.copies[0].wait_recv()

            @pl.when(has_right)
            def _():
                self.copies[1].wait_recv()

        def wait_send(self):
            @pl.when(has_right)
            def _():
                self.copies[0].wait_send()

            @pl.when(has_left)
            def _():
                self.copies[1].wait_send()

    def send_halo(s):
        return Pair(
            (local[s].at[pl.ds(B - 2, 2)], local[s].at[pl.ds(0, 2)]),
            (edge[s].at[0, pl.ds(0, 2)], edge[s].at[1, pl.ds(4, 2)]),
            (halo_s.at[s, 0], halo_s.at[s, 1]),
            (halo_r.at[s, 0], halo_r.at[s, 1]),
        )

    @pl.when(jnp.logical_not(has_left))
    def _():
        for ref in edge:
            ref[0, 0:2] = jnp.zeros((2, FN, R), BF)
        orecv[0] = jnp.full((1, 128), -1, I32)
        vrecv[0] = jnp.zeros((32, 256), BF)

    @pl.when(jnp.logical_not(has_right))
    def _():
        for ref in edge:
            ref[1, 4:6] = jnp.zeros((2, FN, R), BF)
        orecv[1] = jnp.full((1, 128), -1, I32)
        vrecv[1] = jnp.zeros((32, 256), BF)

    near_arrives = jnp.where(core == 1, has_right, has_left)

    @pl.when(jnp.logical_not(near_arrives))
    def _():
        nrecv[...] = jnp.zeros((2, 2, 128), F32)

    part[0, 0:2] = jnp.zeros((2, FN, R), BF)
    part[1, 4:6] = jnp.zeros((2, FN, R), BF)

    loads["psi0"].wait()
    loads["psi1"].wait()
    for i in (0, 1, B - 2, B - 1):
        keep(0, i, psi[i].astype(BF))
    loads["owner"].wait()
    owners = owner[...]
    slot, lane = iota((B, 128), 0), iota((B, 128), 1)
    high = (owners >> 6).astype(F32).astype(BF)
    low = (owners & 63).astype(F32).astype(BF)

    def owner_row(block_row, block_slot):
        pick = jnp.where(slot == block_slot, 1.0, 0.0).astype(BF)
        spread = dot(high, pick) * 64.0 + dot(low, pick)
        return jnp.sum(jnp.where(slot == block_row, spread, 0.0), axis=0, keepdims=True).astype(I32)

    far_owner = owner_row(lane >> 3, 8 + (lane & 7))
    near_owner = owner_row(lane >> 3, lane & 7)
    osend[...] = owner_row(jnp.where((lane & 63) < 32, B - 2, 0) + ((lane >> 4) & 1), lane & 15)

    pl.semaphore_wait(barrier, len(close_peers) + has_right.astype(I32) + has_left.astype(I32))
    halo = send_halo(0)
    o_copies = Pair((osend, osend), (orecv.at[0], orecv.at[1]), (o_s.at[0], o_s.at[1]), (o_r.at[0], o_r.at[1]))
    tell(known1, round1)

    loads["psi"].wait()
    for i in range(2, B - 2):
        keep(0, i, psi[i].astype(BF))

    def blocks(s, rows, read):
        updated = []
        for i in rows:
            nearby = jnp.concatenate([read(i, nbr[k, i] - h * B) for k in range(NBR)], axis=1)
            updated.append((rhs[i] - dot(nearby, couple[i].reshape(NBR * R, R))).astype(BF))
        return [dot(u, diag[i]) for u, i in zip(updated, rows)]

    def from_local(s, i, p):
        return local[s][jnp.clip(p, 0, B - 1)]

    def interior(s, rows):
        return blocks(s, rows, lambda i, p: from_local(s, i, p))

    def from_edge(ref, i, p):
        return ref[0, jnp.clip(p + 2, 0, 5)] if i < 2 else ref[1, jnp.clip(p - (B - 4), 0, 5)]

    def boundary(s):
        return blocks(s, OUTER, lambda i, p: from_edge(edge[s], i, p))

    outs = []

    def put(a, b):
        rows = pl.ds(a, b - a)
        outs.append(pltpu.make_async_copy(adj.at[rows], adj_hbm.at[rows], out_sem.at[len(outs)]))
        outs[-1].start()

    def contributions(rows, values):
        terms = dot(jnp.concatenate([v.astype(BF) for v in values], axis=0), st[...])
        column = iota((FN, 256), 1) % 128 >> 3
        return sum(jnp.where(column == i, terms[FN * n:FN * (n + 1), :], 0.0) for n, i in enumerate(rows))

    loads["nbr"].wait()
    loads["rhs"].wait()
    for group in weights:
        for copy in group:
            copy.wait()
    for i, value in zip(INNER, interior(0, INNER)):
        keep(1, i, value.astype(BF))
    loads["sens"].wait()
    wide = sens[...].astype(F32)
    for q, first in enumerate((8, 0)):
        chunk = wide[:, first:first + 8, :].reshape(128, R)
        st[:, q * 128:(q + 1) * 128] = (-jnp.transpose(chunk)).astype(BF)
    block_of = near_owner >> 4
    group = jnp.where(block_of == h, 0, jnp.where(block_of == h - 1, 4, 8))
    place = group + (near_owner & 3) * 32 + ((near_owner >> 3) & 1) * 2 + ((near_owner >> 2) & 1)
    place = jnp.where(jnp.abs(block_of - h) <= 1, place, -1)
    column = jnp.transpose(jnp.broadcast_to(place, (8, 128)).astype(F32))[:, :1].astype(I32)
    ohn[...] = jnp.where(column == iota((128, 128), 1), 1.0, 0.0).astype(BF)

    for side, (rows, others) in enumerate((((B - 2, B - 1), (B, B + 1)), ((0, 1), (-2, -1)))):
        for n, i in enumerate(rows):
            shape = dot_t(sens[i], diag[i]).astype(BF)
            slots = dot_t(shape, couple[i].reshape(NBR * R, R))
            for m, j in enumerate(others):
                vsend[side, n * KLOC:(n + 1) * KLOC, m * R:(m + 1) * R] = sum(
                    jnp.where(nbr[k, i] - h * B == j, slots[:, k * R:(k + 1) * R], 0.0) for k in range(NBR)
                ).astype(BF)
    v_copies = Pair(*[(ref.at[0], ref.at[1]) for ref in (vsend, vrecv, v_s, v_r)])

    halo.wait_recv()
    sent = [halo, o_copies, v_copies]
    for i, value in zip(OUTER, boundary(0)):
        keep(1, i, value.astype(BF))
    halo = send_halo(1)
    pl.semaphore_wait(known1, len(round1))
    tell(known2, round2)
    o_copies.wait_recv()
    lane = iota((1, 128), 1)
    tgt[0] = jnp.concatenate([far_owner, jnp.where((lane & 63) < 32, orecv[0], orecv[1])], axis=0)
    tgt_copies = [
        remote(tgt.at[0], tgt.at[k], tgt_s.at[k - 1], tgt_r.at[k - 1], p) for k, p in zip(z_steps, z_peers)
    ]

    for i, value in zip(INNER, interior(1, INNER)):
        keep(2, i, value.astype(BF))
    values = interior(2, MIDDLE)
    for i, value in zip(MIDDLE, values):
        adj[i] = value
    put(MIDDLE[0], MIDDLE[-1] + 1)
    terms = contributions(MIDDLE, values)
    pl.semaphore_wait(known2, len(round2))
    tell(known3, round3)
    v_copies.wait_recv()
    zero = jnp.zeros((32, 256), F32)
    vt[...] = jnp.transpose(
        jnp.concatenate(
            [
                jnp.concatenate([vrecv[0].astype(F32), zero], axis=1),
                jnp.concatenate([zero, vrecv[1].astype(F32)], axis=1),
                jnp.zeros((64, 512), F32),
            ],
            axis=0,
        )
    ).astype(BF)

    halo.wait_recv()
    sent.append(halo)
    for i, value in zip(OUTER, boundary(1)):
        keep(2, i, value.astype(BF))
    halo = send_halo(2)

    rows = BETWEEN + OUTER
    values = blocks(2, rows, lambda i, p: from_edge(part, i, p) if i in OUTER else from_local(2, i, p))
    terms = (terms + contributions(rows, values)).astype(BF)
    beyond = dot(jnp.concatenate([local[2][i] for i in OUTER], axis=1), vt[...])
    lane = iota((16, 128), 1)
    crecv[0, 0:FN] = terms[:, :128]
    crecv[0, FN:48] = jnp.where(lane < 64, beyond[:16], pltpu.roll(beyond[16:], 64, 1)).astype(BF)

    c_copies = [remote(crecv.at[0], crecv.at[k], c_s.at[k - 1], c_r.at[k - 1], p) for k, p in zip(z_steps, z_peers)]
    close = dot(terms[:, 128:], ohn[...])
    stacked = jnp.concatenate([close if g == 0 else pltpu.roll(close, 128 - 32 * g, 1) for g in range(4)], axis=0)
    close = jnp.transpose(stacked)[:16, :]
    nsend[0] = close[6:8, :]
    nsend[1] = close[8:10, :]
    n_copies = [
        pltpu.make_async_remote_copy(
            src_ref=nsend.at[k], dst_ref=nrecv.at[core], send_sem=n_s.at[k], recv_sem=n_r.at[core],
            device_id=peer, device_id_type=MESH,
        )
        for k, peer in enumerate(((left[0], 1), (right[0], 0)))
    ]
    for there, copy in zip((has_left, has_right), n_copies):
        @pl.when(there)
        def _():
            copy.start()
    for i, value in zip(BETWEEN, values):
        adj[i] = value
    put(2, 4)
    put(B - 4, B - 2)
    for copy in tgt_copies:
        copy.wait_recv()
    for n in range(2):
        rows = jnp.concatenate([tgt[k, n:n + 1] for k in range(NZ)], axis=0)
        hull = rows >> 4
        place = (rows & 3) * 128 + (hull // NZ) * 4 + ((rows >> 3) & 1) * 2 + ((rows >> 2) & 1)
        place = jnp.where((hull % NZ == z) & (rows >= 0), place, -1)
        if NZ < 8:
            place = jnp.concatenate([place] * (8 // NZ), axis=0)
        columns = jnp.transpose(place.astype(F32)).astype(I32)
        for k in range(NZ):
            oh[(2 * k + n) * 128:(2 * k + n + 1) * 128, :] = jnp.where(
                columns[:, k:k + 1] == iota((128, 512), 1), 1.0, 0.0
            ).astype(BF)
    pl.semaphore_wait(known3, len(round3))
    lane = iota((16, 128), 1)
    dense = None
    arrivals = [None] + c_copies[::-1]
    for k, copy in zip([0] + z_steps[::-1], arrivals):
        if copy is not None:
            copy.wait_recv()
        both = crecv[k, FN:48].astype(F32)
        extra = jnp.concatenate([jnp.where(lane < 64, both, 0.0), jnp.where(lane < 64, 0.0, both)], axis=0)
        terms = jnp.concatenate([crecv[k, 0:FN], extra.astype(BF)], axis=1)
        product = dot(terms, oh[k * 256:(k + 1) * 256, :])
        dense = product if dense is None else dense + product

    packed = jnp.transpose(jnp.concatenate([dense[:, g * 128:(g + 1) * 128] for g in range(4)], axis=0))
    for d in range(2 * NX * NY):
        psend[d] = packed[2 * d:2 * d + 2, :]
    mine = (x * NY + y) * 2
    psend[mine] += close[0:2, :]
    psend[mine + 1] += close[2:4, :]
    p_copies = [
        remote(
            psend.at[(((x + i) % NX) * NY + (y + k) % NY) * 2 + (core + e) % 2],
            precv.at[(e * NX + i) * NY + k], p_s.at[n], p_r.at[n], plane_peers[n],
        )
        for n, (e, i, k) in enumerate(plane)
    ]
    own = psend[mine + core]
    for copy in sent + tgt_copies + c_copies:
        copy.wait_send()
    for there, copy in zip((has_left, has_right), n_copies):
        @pl.when(there)
        def _():
            copy.wait_send()

    @pl.when(near_arrives)
    def _():
        for k in range(2):
            pltpu.make_async_remote_copy(
                src_ref=nsend.at[k], dst_ref=nrecv.at[k], send_sem=n_s.at[k], recv_sem=n_r.at[k],
                device_id=twin[0], device_id_type=MESH,
            ).wait_recv()

    halo.wait_recv()
    for i, value in zip(OUTER, boundary(2)):
        adj[i] = value
    put(0, 2)
    put(B - 2, B)
    halo.wait_send()
    for copy in p_copies:
        copy.wait_send()
    for copy in p_copies[::-1]:
        copy.wait_recv()
    half = NX * NY
    halves = [own + jnp.sum(precv[1:half], axis=0), jnp.sum(precv[half:2 * half], axis=0)]
    ordered = (
        jnp.where(core == 0, halves[0], halves[1]) + nrecv[0],
        jnp.where(core == 0, halves[1], halves[0]) + nrecv[1],
    )
    row, lane = iota((8, 128), 0), iota((8, 128), 1)
    wide = [jnp.where(row < 4, half[0:1], half[1:2]) for half in ordered]
    result = jnp.zeros((8, 128), F32)
    for g in range(4):
        first = wide[0] if g == 0 else pltpu.roll(wide[0], 128 - 32 * g, 1)
        second = wide[1] if g == 1 else pltpu.roll(wide[1], (160 - 32 * g) % 128, 1)
        result = jnp.where((row & 3) == g, jnp.where(lane < FN, first, second), result)
    grad_ref[...] = result[:, :2 * FN]

    for copy in outs:
        copy.wait()


def emit(adj_in, grad_in, adj_out, grad_out, sem):
    copies = [
        pltpu.make_async_copy(adj_in, adj_out, sem.at[0]),
        pltpu.make_async_copy(grad_in, grad_out, sem.at[1]),
    ]
    for copy in copies:
        copy.start()
    for copy in copies:
        copy.wait()


def shards(adj_rhs, psi_init, couple, diag_inv, neighbours, sens, owner):
    vmem, dma = pltpu.VMEM, pltpu.SemaphoreType.DMA
    pinned = (pltpu.VMEM((B, FN, R), F32), pltpu.VMEM((8, 2 * FN), F32))
    shapes = (jax.ShapeDtypeStruct((B, FN, R), F32), jax.ShapeDtypeStruct((8, 2 * FN), F32))
    results = pl.pallas_call(
        kernel,
        out_shape=pinned,
        in_specs=[pl.BlockSpec(memory_space=pltpu.HBM)] * 7,
        out_specs=(pl.BlockSpec(memory_space=pl.ANY), pl.BlockSpec(memory_space=pltpu.VMEM)),
        scratch_shapes=[
            vmem((B, FN, R), F32),
            vmem((B, FN, R), F32),
            vmem((B, NBR, R, R), BF),
            vmem((B, R, R), BF),
            pltpu.SMEM((NBR, B), I32),
            vmem((B, KLOC, R), BF),
            vmem((B, KLOC), I32),
            vmem((B, FN, R), F32),
            *[vmem((B, FN, R), BF)] * SWEEPS,
            *[vmem((2, 6, FN, R), BF)] * SWEEPS,
            vmem((2, 6, FN, R), BF),
            vmem((R, 256), BF),
            vmem((1, 128), I32),
            vmem((2, 1, 128), I32),
            vmem((2, 32, 256), BF),
            vmem((2, 32, 256), BF),
            vmem((512, 128), BF),
            vmem((NZ, 2, 128), I32),
            vmem((2 * NZ * 128, 512), BF),
            vmem((128, 128), BF),
            vmem((NZ, 48, 128), BF),
            vmem((2, 2, 128), F32),
            vmem((2, 2, 128), F32),
            vmem((64, 2, 128), F32),
            vmem((2 * NX * NY, 2, 128), F32),
            dma((7,)), dma((2 * len(GROUPS),)), dma((5,)),
            dma((SWEEPS, 2)), dma((SWEEPS, 2)),
            dma((2,)), dma((2,)), dma((2,)), dma((2,)),
            dma((NZ - 1,)), dma((NZ - 1,)), dma((NZ - 1,)), dma((NZ - 1,)),
            dma((2,)), dma((2,)),
            dma((2 * NX * NY - 1,)), dma((2 * NX * NY - 1,)),
            *[pltpu.SemaphoreType.REGULAR] * 3,
        ],
        compiler_params=pltpu.CompilerParams(
            collective_id=0, has_side_effects=True, vmem_limit_bytes=62 * 2**20
        ),
        name="adjoint_gradient",
    )(adj_rhs, psi_init, couple, diag_inv, neighbours.T, sens, owner)
    return pl.pallas_call(
        emit,
        out_shape=shapes,
        in_specs=[pl.BlockSpec(memory_space=pl.ANY)] * 2,
        out_specs=(pl.BlockSpec(memory_space=pl.ANY),) * 2,
        scratch_shapes=[dma((2,))],
        compiler_params=pltpu.CompilerParams(vmem_limit_bytes=24 * 2**20),
        name="emit",
    )(*results)


def solution(mesh):
    return jax.shard_map(
        shards,
        mesh=mesh,
        in_specs=(
            P("hull", "fn", None),
            P("hull", "fn", None),
            P("hull", None, None, None),
            P("hull", None, None),
            P("hull", None),
            P("hull", None, None),
            P("hull", None),
        ),
        out_specs=(P("hull", "fn", None), P(("hull", "fn"), None)),
        check_vma=False,
    )
```

```python
import functools

import jax
import jax.numpy as jnp
from jax import lax
from jax.experimental import pallas as pl
from jax.experimental.pallas import tpu as pltpu
from jax.sharding import PartitionSpec as P

MESH = pl.DeviceIdType.MESH
BF, F32, I32 = jnp.bfloat16, jnp.float32, jnp.int32
NX, NY, NZ = 4, 8, 8
B = 16
FN = 32
R = 128
NBR, KLOC, SWEEPS, REACH = 6, 16, 3, 2
GROUPS = ((2, 6), (6, 10), (10, 14), (0, 2), (14, 16))
INNER = tuple(range(2, B - 2))
MIDDLE = tuple(range(4, B - 4))
BETWEEN = (2, 3, B - 4, B - 3)
OUTER = (0, 1, B - 2, B - 1)


def dot(a, b):
    return jnp.dot(a, b, preferred_element_type=F32)


def dot_t(a, b):
    return lax.dot_general(a, b, (((1,), (1,)), ((), ())), preferred_element_type=F32)


def iota(shape, dim):
    return lax.broadcasted_iota(I32, shape, dim)


def kernel(
    rhs_hbm, psi_hbm, couple_hbm, diag_hbm, nbr_hbm, sens_hbm, owner_hbm,
    adj_hbm, grad_ref,
    rhs, psi, couple, diag, nbr, sens, owner, adj,
    local0, local1, local2, edge0, edge1, edge2, part, st, osend, orecv, vsend, vrecv, vt,
    tgt, oh, ohn, crecv, nsend, nrecv, psend, precv,
    load_sem, weight_sem, out_sem, halo_s, halo_r, o_s, o_r, v_s, v_r, tgt_s, tgt_r, c_s, c_r, n_s, n_r, p_s, p_r,
    known1, known2, known3, known4,
):
    local, edge = (local0, local1, local2), (edge0, edge1, edge2)
    h = lax.axis_index("hull")
    core = lax.axis_index("fn")
    n_hull = NX * NY * NZ
    x, y, z = h // (NY * NZ), (h // NZ) % NY, h % NZ

    def device(i, j, k, c):
        return ((i * NY + j) * NZ + k, c)

    has_left, has_right = h > 0, h < n_hull - 1
    left, right = (jnp.maximum(h - 1, 0), core), (jnp.minimum(h + 1, n_hull - 1), core)
    z_steps = sorted(range(1, NZ), key=lambda k: -min(k, NZ - k))
    z_peers = [device(x, y, (z + k) % NZ, core) for k in z_steps]
    x_peers = [device((x + k) % NX, y, z, core) for k in range(1, NX)]
    plane = [(e, i, k) for e in range(2) for i in range(NX) for k in range(NY) if (e, i, k) != (0, 0, 0)]
    plane.sort(key=lambda t: (-min(t[1], NX - t[1]) - min(t[2], NY - t[2]), -t[0]))
    plane_peers = [device((x + i) % NX, (y + k) % NY, z, (core + e) % 2) for e, i, k in plane]
    twin = [(h, 1 - core)]

    def within(n, far):
        return [k for k in range(1, n) if min(k, n - k) in far]

    def along(far):
        steps_z = [device(x, y, (z + k) % NZ, core) for k in within(NZ, far)]
        return steps_z + [device(x, (y + k) % NY, z, core) for k in within(NY, far)]

    def tell(semaphore, peers):
        for peer in peers:
            pl.semaphore_signal(semaphore, inc=1, device_id=peer, device_id_type=MESH)

    barrier = pltpu.get_barrier_semaphore()
    for there, peer in ((has_right, right), (has_left, left)):
        @pl.when(there)
        def _():
            tell(barrier, [peer])
    next_peers = along((1,)) + [device((x + k) % NX, y, z, core) for k in within(NX, (1,))]
    close_peers = next_peers + twin
    tell(barrier, close_peers)
    round1, round2, round3, round4 = next_peers, along((2,)) + twin, x_peers + twin, x_peers

    loads = {}

    def load(name, source, target):
        loads[name] = pltpu.make_async_copy(source, target, load_sem.at[len(loads)])
        loads[name].start()

    load("psi0", psi_hbm.at[pl.ds(0, 2)], psi.at[pl.ds(0, 2)])
    load("psi1", psi_hbm.at[pl.ds(B - 2, 2)], psi.at[pl.ds(B - 2, 2)])
    load("owner", owner_hbm, owner)
    load("psi", psi_hbm.at[pl.ds(2, B - 4)], psi.at[pl.ds(2, B - 4)])
    load("nbr", nbr_hbm, nbr)
    load("rhs", rhs_hbm, rhs)
    weights = []
    for g, (a, b) in enumerate(GROUPS):
        rows = pl.ds(a, b - a)
        weights.append((
            pltpu.make_async_copy(couple_hbm.at[rows], couple.at[rows], weight_sem.at[2 * g]),
            pltpu.make_async_copy(diag_hbm.at[rows], diag.at[rows], weight_sem.at[2 * g + 1]),
        ))
        for copy in weights[-1]:
            copy.start()
        if g == 0:
            load("sens", sens_hbm, sens)

    def remote(source, target, send, recv, peer):
        copy = pltpu.make_async_remote_copy(
            src_ref=source, dst_ref=target, send_sem=send, recv_sem=recv, device_id=peer, device_id_type=MESH
        )
        copy.start()
        return copy

    def keep(s, i, value):
        local[s][i] = value
        if i < 4:
            edge[s][0, i + 2] = value
            if s == SWEEPS - 1:
                part[0, i + 2] = value
        if i >= B - 4:
            edge[s][1, i - (B - 4)] = value
            if s == SWEEPS - 1:
                part[1, i - (B - 4)] = value

    class Pair:
        def __init__(self, sources, targets, send, recv):
            self.copies = [
                pltpu.make_async_remote_copy(
                    src_ref=sources[k], dst_ref=targets[k], send_sem=send[k], recv_sem=recv[k],
                    device_id=(right, left)[k], device_id_type=MESH,
                )
                for k in range(2)
            ]

            @pl.when(has_right)
            def _():
                self.copies[0].start()

            @pl.when(has_left)
            def _():
                self.copies[1].start()

        def wait_recv(self):
            @pl.when(has_left)
            def _():
                self.copies[0].wait_recv()

            @pl.when(has_right)
            def _():
                self.copies[1].wait_recv()

        def wait_send(self):
            @pl.when(has_right)
            def _():
                self.copies[0].wait_send()

            @pl.when(has_left)
            def _():
                self.copies[1].wait_send()

    def send_halo(s):
        return Pair(
            (local[s].at[pl.ds(B - 2, 2)], local[s].at[pl.ds(0, 2)]),
            (edge[s].at[0, pl.ds(0, 2)], edge[s].at[1, pl.ds(4, 2)]),
            (halo_s.at[s, 0], halo_s.at[s, 1]),
            (halo_r.at[s, 0], halo_r.at[s, 1]),
        )

    @pl.when(jnp.logical_not(has_left))
    def _():
        for ref in edge:
            ref[0, 0:2] = jnp.zeros((2, FN, R), BF)
        orecv[0] = jnp.full((1, 128), -1, I32)
        vrecv[0] = jnp.zeros((32, 256), BF)

    @pl.when(jnp.logical_not(has_right))
    def _():
        for ref in edge:
            ref[1, 4:6] = jnp.zeros((2, FN, R), BF)
        orecv[1] = jnp.full((1, 128), -1, I32)
        vrecv[1] = jnp.zeros((32, 256), BF)

    near_arrives = jnp.where(core == 1, has_right, has_left)

    @pl.when(jnp.logical_not(near_arrives))
    def _():
        nrecv[...] = jnp.zeros((2, 2, 128), F32)

    part[0, 0:2] = jnp.zeros((2, FN, R), BF)
    part[1, 4:6] = jnp.zeros((2, FN, R), BF)

    loads["psi0"].wait()
    loads["psi1"].wait()
    for i in (0, 1, B - 2, B - 1):
        keep(0, i, psi[i].astype(BF))
    loads["owner"].wait()
    owners = owner[...]
    slot, lane = iota((B, 128), 0), iota((B, 128), 1)
    high = (owners >> 6).astype(F32).astype(BF)
    low = (owners & 63).astype(F32).astype(BF)

    def owner_row(block_row, block_slot):
        pick = jnp.where(slot == block_slot, 1.0, 0.0).astype(BF)
        spread = dot(high, pick) * 64.0 + dot(low, pick)
        return jnp.sum(jnp.where(slot == block_row, spread, 0.0), axis=0, keepdims=True).astype(I32)

    far_owner = owner_row(lane >> 3, 8 + (lane & 7))
    near_owner = owner_row(lane >> 3, lane & 7)
    osend[...] = owner_row(jnp.where((lane & 63) < 32, B - 2, 0) + ((lane >> 4) & 1), lane & 15)

    pl.semaphore_wait(barrier, len(close_peers) + has_right.astype(I32) + has_left.astype(I32))
    halo = send_halo(0)
    o_copies = Pair((osend, osend), (orecv.at[0], orecv.at[1]), (o_s.at[0], o_s.at[1]), (o_r.at[0], o_r.at[1]))
    tell(known1, round1)

    loads["psi"].wait()
    for i in range(2, B - 2):
        keep(0, i, psi[i].astype(BF))

    def blocks(s, rows, read):
        updated = []
        for i in rows:
            nearby = jnp.concatenate([read(i, nbr[k, i] - h * B) for k in range(NBR)], axis=1)
            updated.append((rhs[i] - dot(nearby, couple[i].reshape(NBR * R, R))).astype(BF))
        return [dot(u, diag[i]) for u, i in zip(updated, rows)]

    def from_local(s, i, p):
        return local[s][jnp.clip(p, 0, B - 1)]

    def interior(s, rows):
        return blocks(s, rows, lambda i, p: from_local(s, i, p))

    def from_edge(ref, i, p):
        return ref[0, jnp.clip(p + 2, 0, 5)] if i < 2 else ref[1, jnp.clip(p - (B - 4), 0, 5)]

    def boundary(s):
        return blocks(s, OUTER, lambda i, p: from_edge(edge[s], i, p))

    outs = []

    def put(a, b):
        rows = pl.ds(a, b - a)
        outs.append(pltpu.make_async_copy(adj.at[rows], adj_hbm.at[rows], out_sem.at[len(outs)]))
        outs[-1].start()

    def contributions(rows, values):
        terms = dot(jnp.concatenate([v.astype(BF) for v in values], axis=0), st[...])
        column = iota((FN, 256), 1) % 128 >> 3
        return sum(jnp.where(column == i, terms[FN * n:FN * (n + 1), :], 0.0) for n, i in enumerate(rows))

    loads["nbr"].wait()
    loads["rhs"].wait()
    for group in weights:
        for copy in group:
            copy.wait()
    for i, value in zip(INNER, interior(0, INNER)):
        keep(1, i, value.astype(BF))
    loads["sens"].wait()
    wide = sens[...].astype(F32)
    for q, first in enumerate((8, 0)):
        chunk = wide[:, first:first + 8, :].reshape(128, R)
        st[:, q * 128:(q + 1) * 128] = (-jnp.transpose(chunk)).astype(BF)
    block_of = near_owner >> 4
    group = jnp.where(block_of == h, 0, jnp.where(block_of == h - 1, 4, 8))
    place = group + (near_owner & 3) * 32 + ((near_owner >> 3) & 1) * 2 + ((near_owner >> 2) & 1)
    place = jnp.where(jnp.abs(block_of - h) <= 1, place, -1)
    column = jnp.transpose(jnp.broadcast_to(place, (8, 128)).astype(F32))[:, :1].astype(I32)
    ohn[...] = jnp.where(column == iota((128, 128), 1), 1.0, 0.0).astype(BF)

    for side, (rows, others) in enumerate((((B - 2, B - 1), (B, B + 1)), ((0, 1), (-2, -1)))):
        for n, i in enumerate(rows):
            shape = dot_t(sens[i], diag[i]).astype(BF)
            slots = dot_t(shape, couple[i].reshape(NBR * R, R))
            for m, j in enumerate(others):
                vsend[side, n * KLOC:(n + 1) * KLOC, m * R:(m + 1) * R] = sum(
                    jnp.where(nbr[k, i] - h * B == j, slots[:, k * R:(k + 1) * R], 0.0) for k in range(NBR)
                ).astype(BF)
    v_copies = Pair(*[(ref.at[0], ref.at[1]) for ref in (vsend, vrecv, v_s, v_r)])

    pl.semaphore_wait(known1, len(round1))
    tell(known2, round2)
    halo.wait_recv()
    sent = [halo, o_copies, v_copies]
    for i, value in zip(OUTER, boundary(0)):
        keep(1, i, value.astype(BF))
    halo = send_halo(1)
    for i, value in zip(INNER, interior(1, INNER)):
        keep(2, i, value.astype(BF))
    values = interior(2, MIDDLE)
    for i, value in zip(MIDDLE, values):
        adj[i] = value
    put(MIDDLE[0], MIDDLE[-1] + 1)
    terms = contributions(MIDDLE, values)
    v_copies.wait_recv()
    zero = jnp.zeros((32, 256), F32)
    vt[...] = jnp.transpose(
        jnp.concatenate(
            [
                jnp.concatenate([vrecv[0].astype(F32), zero], axis=1),
                jnp.concatenate([zero, vrecv[1].astype(F32)], axis=1),
                jnp.zeros((64, 512), F32),
            ],
            axis=0,
        )
    ).astype(BF)

    pl.semaphore_wait(known2, len(round2))
    tell(known3, round3)
    o_copies.wait_recv()
    lane = iota((1, 128), 1)
    tgt[0] = jnp.concatenate([far_owner, jnp.where((lane & 63) < 32, orecv[0], orecv[1])], axis=0)
    tgt_copies = [
        remote(tgt.at[0], tgt.at[k], tgt_s.at[k - 1], tgt_r.at[k - 1], p) for k, p in zip(z_steps, z_peers)
    ]

    halo.wait_recv()
    sent.append(halo)
    for i, value in zip(OUTER, boundary(1)):
        keep(2, i, value.astype(BF))

    rows = BETWEEN + OUTER
    values = blocks(2, rows, lambda i, p: from_edge(part, i, p) if i in OUTER else from_local(2, i, p))
    terms = (terms + contributions(rows, values)).astype(BF)
    beyond = dot(jnp.concatenate([local[2][i] for i in OUTER], axis=1), vt[...])
    lane = iota((16, 128), 1)
    crecv[0, 0:FN] = terms[:, :128]
    crecv[0, FN:48] = jnp.where(lane < 64, beyond[:16], pltpu.roll(beyond[16:], 64, 1)).astype(BF)

    c_copies = [remote(crecv.at[0], crecv.at[k], c_s.at[k - 1], c_r.at[k - 1], p) for k, p in zip(z_steps, z_peers)]
    close = dot(terms[:, 128:], ohn[...])
    stacked = jnp.concatenate([close if g == 0 else pltpu.roll(close, 128 - 32 * g, 1) for g in range(4)], axis=0)
    close = jnp.transpose(stacked)[:16, :]
    nsend[0] = close[6:8, :]
    nsend[1] = close[8:10, :]
    n_copies = [
        pltpu.make_async_remote_copy(
            src_ref=nsend.at[k], dst_ref=nrecv.at[core], send_sem=n_s.at[k], recv_sem=n_r.at[core],
            device_id=peer, device_id_type=MESH,
        )
        for k, peer in enumerate(((left[0], 1), (right[0], 0)))
    ]
    for there, copy in zip((has_left, has_right), n_copies):
        @pl.when(there)
        def _():
            copy.start()
    halo = send_halo(2)
    for i, value in zip(BETWEEN, values):
        adj[i] = value
    put(2, 4)
    put(B - 4, B - 2)
    pl.semaphore_wait(known3, len(round3))
    tell(known4, round4)
    for copy in tgt_copies:
        copy.wait_recv()
    for n in range(2):
        rows = jnp.concatenate([tgt[k, n:n + 1] for k in range(NZ)], axis=0)
        hull = rows >> 4
        place = (rows & 3) * 128 + (hull // NZ) * 4 + ((rows >> 3) & 1) * 2 + ((rows >> 2) & 1)
        place = jnp.where((hull % NZ == z) & (rows >= 0), place, -1)
        if NZ < 8:
            place = jnp.concatenate([place] * (8 // NZ), axis=0)
        columns = jnp.transpose(place.astype(F32)).astype(I32)
        for k in range(NZ):
            oh[(2 * k + n) * 128:(2 * k + n + 1) * 128, :] = jnp.where(
                columns[:, k:k + 1] == iota((128, 512), 1), 1.0, 0.0
            ).astype(BF)
    lane = iota((16, 128), 1)
    dense = None
    arrivals = [None] + c_copies[::-1]
    for k, copy in zip([0] + z_steps[::-1], arrivals):
        if copy is not None:
            copy.wait_recv()
        both = crecv[k, FN:48].astype(F32)
        extra = jnp.concatenate([jnp.where(lane < 64, both, 0.0), jnp.where(lane < 64, 0.0, both)], axis=0)
        terms = jnp.concatenate([crecv[k, 0:FN], extra.astype(BF)], axis=1)
        product = dot(terms, oh[k * 256:(k + 1) * 256, :])
        dense = product if dense is None else dense + product

    packed = jnp.transpose(jnp.concatenate([dense[:, g * 128:(g + 1) * 128] for g in range(4)], axis=0))
    for d in range(2 * NX * NY):
        psend[d] = packed[2 * d:2 * d + 2, :]
    mine = (x * NY + y) * 2
    psend[mine] += close[0:2, :]
    psend[mine + 1] += close[2:4, :]
    pl.semaphore_wait(known4, len(round4))
    p_copies = [
        remote(
            psend.at[(((x + i) % NX) * NY + (y + k) % NY) * 2 + (core + e) % 2],
            precv.at[(e * NX + i) * NY + k], p_s.at[n], p_r.at[n], plane_peers[n],
        )
        for n, (e, i, k) in enumerate(plane)
    ]
    own = psend[mine + core]
    for copy in sent + tgt_copies + c_copies:
        copy.wait_send()
    for there, copy in zip((has_left, has_right), n_copies):
        @pl.when(there)
        def _():
            copy.wait_send()

    @pl.when(near_arrives)
    def _():
        for k in range(2):
            pltpu.make_async_remote_copy(
                src_ref=nsend.at[k], dst_ref=nrecv.at[k], send_sem=n_s.at[k], recv_sem=n_r.at[k],
                device_id=twin[0], device_id_type=MESH,
            ).wait_recv()

    halo.wait_recv()
    for i, value in zip(OUTER, boundary(2)):
        adj[i] = value
    put(0, 2)
    put(B - 2, B)
    halo.wait_send()
    for copy in p_copies:
        copy.wait_send()
    for copy in p_copies[::-1]:
        copy.wait_recv()
    half = NX * NY
    halves = [own + jnp.sum(precv[1:half], axis=0), jnp.sum(precv[half:2 * half], axis=0)]
    ordered = (
        jnp.where(core == 0, halves[0], halves[1]) + nrecv[0],
        jnp.where(core == 0, halves[1], halves[0]) + nrecv[1],
    )
    row, lane = iota((8, 128), 0), iota((8, 128), 1)
    wide = [jnp.where(row < 4, half[0:1], half[1:2]) for half in ordered]
    result = jnp.zeros((8, 128), F32)
    for g in range(4):
        first = wide[0] if g == 0 else pltpu.roll(wide[0], 128 - 32 * g, 1)
        second = wide[1] if g == 1 else pltpu.roll(wide[1], (160 - 32 * g) % 128, 1)
        result = jnp.where((row & 3) == g, jnp.where(lane < FN, first, second), result)
    grad_ref[...] = result[:, :2 * FN]

    for copy in outs:
        copy.wait()


def emit(adj_in, grad_in, adj_out, grad_out, sem):
    copies = [
        pltpu.make_async_copy(adj_in, adj_out, sem.at[0]),
        pltpu.make_async_copy(grad_in, grad_out, sem.at[1]),
    ]
    for copy in copies:
        copy.start()
    for copy in copies:
        copy.wait()


def shards(adj_rhs, psi_init, couple, diag_inv, neighbours, sens, owner):
    vmem, dma = pltpu.VMEM, pltpu.SemaphoreType.DMA
    pinned = (pltpu.VMEM((B, FN, R), F32), pltpu.VMEM((8, 2 * FN), F32))
    shapes = (jax.ShapeDtypeStruct((B, FN, R), F32), jax.ShapeDtypeStruct((8, 2 * FN), F32))
    results = pl.pallas_call(
        kernel,
        out_shape=pinned,
        in_specs=[pl.BlockSpec(memory_space=pltpu.HBM)] * 7,
        out_specs=(pl.BlockSpec(memory_space=pl.ANY), pl.BlockSpec(memory_space=pltpu.VMEM)),
        scratch_shapes=[
            vmem((B, FN, R), F32),
            vmem((B, FN, R), F32),
            vmem((B, NBR, R, R), BF),
            vmem((B, R, R), BF),
            pltpu.SMEM((NBR, B), I32),
            vmem((B, KLOC, R), BF),
            vmem((B, KLOC), I32),
            vmem((B, FN, R), F32),
            *[vmem((B, FN, R), BF)] * SWEEPS,
            *[vmem((2, 6, FN, R), BF)] * SWEEPS,
            vmem((2, 6, FN, R), BF),
            vmem((R, 256), BF),
            vmem((1, 128), I32),
            vmem((2, 1, 128), I32),
            vmem((2, 32, 256), BF),
            vmem((2, 32, 256), BF),
            vmem((512, 128), BF),
            vmem((NZ, 2, 128), I32),
            vmem((2 * NZ * 128, 512), BF),
            vmem((128, 128), BF),
            vmem((NZ, 48, 128), BF),
            vmem((2, 2, 128), F32),
            vmem((2, 2, 128), F32),
            vmem((64, 2, 128), F32),
            vmem((2 * NX * NY, 2, 128), F32),
            dma((7,)), dma((2 * len(GROUPS),)), dma((5,)),
            dma((SWEEPS, 2)), dma((SWEEPS, 2)),
            dma((2,)), dma((2,)), dma((2,)), dma((2,)),
            dma((NZ - 1,)), dma((NZ - 1,)), dma((NZ - 1,)), dma((NZ - 1,)),
            dma((2,)), dma((2,)),
            dma((2 * NX * NY - 1,)), dma((2 * NX * NY - 1,)),
            *[pltpu.SemaphoreType.REGULAR] * 4,
        ],
        compiler_params=pltpu.CompilerParams(
            collective_id=0, has_side_effects=True, vmem_limit_bytes=62 * 2**20
        ),
        name="adjoint_gradient",
    )(adj_rhs, psi_init, couple, diag_inv, neighbours.T, sens, owner)
    return pl.pallas_call(
        emit,
        out_shape=shapes,
        in_specs=[pl.BlockSpec(memory_space=pl.ANY)] * 2,
        out_specs=(pl.BlockSpec(memory_space=pl.ANY),) * 2,
        scratch_shapes=[dma((2,))],
        compiler_params=pltpu.CompilerParams(vmem_limit_bytes=24 * 2**20),
        name="emit",
    )(*results)


def solution(mesh):
    return jax.shard_map(
        shards,
        mesh=mesh,
        in_specs=(
            P("hull", "fn", None),
            P("hull", "fn", None),
            P("hull", None, None, None),
            P("hull", None, None),
            P("hull", None),
            P("hull", None, None),
            P("hull", None),
        ),
        out_specs=(P("hull", "fn", None), P(("hull", "fn"), None)),
        check_vma=False,
    )
```
